32 devices in a mesh: groups: 2 (over y), store: 4 (over x, core), tensor: 4 (over z).
Axes of the slice: x: 2, y: 2, z: 4, core: 2. Of those that a mesh axis runs over, the one named last changes fastest.
Arguments:
- normed_hidden_rows: bfloat16 [8192, 8192], P(('groups', 'store', 'tensor')), parts along dimension 0, may hold values from -6 to 6
- base_query_weight: bfloat16 [8192, 8192], P('tensor'), may hold values from -0.0625 to 0.0625
- adapter_down_maps: bfloat16 [128, 64, 8192], P('store', None, 'tensor'), may hold values from -0.0625 to 0.0625
- adapter_up_maps: bfloat16 [128, 64, 8192], P('store', None, 'tensor'), may hold values from -0.75 to 0.75
- row_adapter_ids: int32 [8192], P('groups'), parts along dimension 0, may hold values from 0 to 127, as said below
- adapter_store_slot: int32 [128], replicated, may hold values from 0 to 127, each once
Outputs:
- queries: bfloat16 [8192, 8192], P(('groups', 'store', 'tensor')), parts along dimension 0
The draws below stay inside these ranges and needn't reach their ends.
There are 2 independent parts, one for each index of `groups`. The reference program is written for one: setup_inputs(seed, part) draws one part's arguments, and reference() takes and returns one part's arrays. A program takes and returns all parts, laid end to end along the dimension named above; an argument that names none is the same for every part. Nothing has to cross between parts.
Inputs may be any that keep to these rules, and one draw needn't show every extreme that they name: `row_adapter_ids`: constant over each aligned block of 128 rows. `adapter_store_slot`: each slot once.
All inputs are finite; a program needn't handle non-finite values.
Results may differ from the reference program's by a relative error of at most 0.014.
Values may be sent and summed in bfloat16 or wider, within the bound.
No kernel may reach another device: no remote copies, remote signals or barrier semaphores. Data moves between devices by JAX's collectives and lax.ppermute only.
A program may use at most 256 MiB of HBM per device.

```python
import jax
import jax.numpy as jnp
from jax import lax

MODEL_WIDTH = 8192
ADAPTER_RANK = 64
TILE = 128
ROWS = 4096
ADAPTER_TOTAL = 128
N_TENSOR = 4


def draw_row_adapter_ids(key, part):
    key = jax.random.fold_in(key, 7)
    first_key, second_key, place_key = jax.random.split(key, 3)
    tiles = ROWS // TILE
    first = jax.random.randint(first_key, (tiles,), 0, ADAPTER_TOTAL)
    second = jax.random.randint(second_key, (tiles,), 0, ADAPTER_TOTAL)
    picked = first * (second + 1) // ADAPTER_TOTAL
    places = jax.random.permutation(place_key, tiles)
    picked = picked.at[places[0]].set(ADAPTER_TOTAL - 1)
    picked = picked.at[places[1]].set(0)
    return jnp.repeat(picked, TILE).astype(jnp.int32)


def level_of(stream_key, extent, cuts, low, largest):
    factor_of, own = 1.0, jax.random.fold_in(stream_key, 6)
    for axis_at, shards_of in cuts:
        steps = jnp.exp(jax.random.uniform(jax.random.fold_in(own, axis_at), (shards_of,), jnp.float32, low / len(cuts), largest / len(cuts)))
        factor_of = factor_of * jnp.repeat(steps, extent[axis_at] // shards_of).reshape([-1 if axis == axis_at else 1 for axis in range(len(extent))])
    return factor_of


def normal_values(rng, shape, spread, most, pieces=(), kind=jnp.bfloat16):
    values = spread * jax.random.normal(rng, shape, jnp.float32)
    if pieces:
        values = values * level_of(rng, shape, pieces, -0.22, 0.18)
    return jnp.clip(values, -most, most).astype(kind)


def setup_inputs(seed: int = 0, part: int = 0) -> dict:
    arg_keys = jax.random.split(jax.random.key(seed), 7)
    part_splits = jax.random.split(jax.random.fold_in(arg_keys[6], part), 7)
    return {
        "normed_hidden_rows": normal_values(part_splits[0], (ROWS, MODEL_WIDTH), 1.0, 6.0, ((0, 16),)),
        "base_query_weight": normal_values(arg_keys[1], (MODEL_WIDTH, MODEL_WIDTH), MODEL_WIDTH ** -0.5, 0.0625, ((0, 4),)),
        "adapter_down_maps": normal_values(arg_keys[2], (ADAPTER_TOTAL, ADAPTER_RANK, MODEL_WIDTH), MODEL_WIDTH ** -0.5, 0.0625, ((0, 4), (2, 4))),
        "adapter_up_maps": normal_values(arg_keys[3], (ADAPTER_TOTAL, ADAPTER_RANK, MODEL_WIDTH), ADAPTER_RANK ** -0.5, 0.75, ((0, 4), (2, 4))),
        "row_adapter_ids": draw_row_adapter_ids(jax.random.fold_in(jax.random.fold_in(arg_keys[6], part), 71), part),
        "adapter_store_slot": jax.random.permutation(arg_keys[5], ADAPTER_TOTAL).astype(jnp.int32),
    }


def reference(normed_hidden_rows, base_query_weight, adapter_down_maps, adapter_up_maps, row_adapter_ids, adapter_store_slot):
    feat = MODEL_WIDTH // N_TENSOR

    def add_part(total, block):
        start = (block * feat).astype(jnp.int32)
        cols = lax.dynamic_slice_in_dim(normed_hidden_rows, start, feat, 1)
        wrows = lax.dynamic_slice_in_dim(base_query_weight, start, feat, 0)
        part = jnp.dot(cols, wrows, preferred_element_type=jnp.float32).astype(jnp.bfloat16)
        part = lax.optimization_barrier(part)
        return total + part.astype(jnp.float32), None

    base, _ = lax.scan(add_part, jnp.zeros((ROWS, MODEL_WIDTH), jnp.float32), jnp.arange(N_TENSOR, dtype=jnp.int32))
    tile_ids = row_adapter_ids.reshape(-1, TILE)[:, 0]
    store_slots = adapter_store_slot[tile_ids]
    down_matrix = adapter_down_maps[store_slots].astype(jnp.float32)
    up_matrix = adapter_up_maps[store_slots].astype(jnp.float32)
    tiled_rows = normed_hidden_rows.reshape(-1, TILE, MODEL_WIDTH).astype(jnp.float32)
    low = jnp.einsum('tnd,trd->tnr', tiled_rows, down_matrix)
    low_b = low.astype(jnp.bfloat16).astype(jnp.float32)
    delta = jnp.einsum('tnr,trd->tnd', low_b, up_matrix).astype(jnp.bfloat16).reshape(ROWS, MODEL_WIDTH)
    return (base + delta.astype(jnp.float32)).astype(jnp.bfloat16)
```

```python
import jax
import jax.numpy as jnp
from jax import lax
from jax.sharding import PartitionSpec as P

TILE = 128
F32 = jnp.float32
BF16 = jnp.bfloat16


def xor_perm(x, axis, d):
    return lax.ppermute(x, axis, [(i, i ^ d) for i in range(lax.axis_size(axis))])


def pick(bank, first, slots):
    count = bank.shape[0]
    held = (slots >= first) & (slots < first + count)
    return jnp.take(bank, jnp.clip(slots - first, 0, count - 1), axis=0), held[:, None, None]


def fetch_maps(bank, slots, me):
    n = lax.axis_size("store")
    first = me * bank.shape[0]
    if n != 4:
        return jnp.take(lax.all_gather(bank, "store", axis=0, tiled=True), slots[me], axis=0)
    own, own_held = pick(bank, first, slots[me])
    mate, _ = pick(bank, first, slots[me ^ 1])
    far, far_held = pick(bank, first, slots[me ^ 2])
    far_mate, _ = pick(bank, first, slots[me ^ 3])
    from_mate = xor_perm(mate, "store", 1)
    far_from_mate = xor_perm(far_mate, "store", 1)
    from_far = xor_perm(jnp.where(far_held, far, far_from_mate), "store", 2)
    mate_first = (me ^ 1) * bank.shape[0]
    mate_held = (slots[me] >= mate_first) & (slots[me] < mate_first + bank.shape[0])
    return jnp.where(own_held, own, jnp.where(mate_held[:, None, None], from_mate, from_far))


def body(x, w, down, up, ids, slot_of):
    stores = lax.axis_size("store")
    n = lax.axis_size("tensor")
    si = lax.axis_index("store")
    ti = lax.axis_index("tensor")
    rows = x.shape[0]
    feat = w.shape[0]
    slots = slot_of[ids.reshape(-1, TILE)[:, 0]].reshape(stores, -1)
    tiles = slots.shape[1]
    blocks = x.reshape(rows, n, feat).transpose(1, 0, 2)
    blocks = lax.all_to_all(blocks, "tensor", split_axis=0, concat_axis=0, tiled=True)
    local = blocks.reshape(n * rows, feat)
    tile_down = fetch_maps(down, slots, si)
    tile_up = fetch_maps(up, slots, si)
    low = jnp.einsum("tnd,trd->tnr", local.reshape(tiles, TILE, feat), tile_down, preferred_element_type=F32)
    low = lax.psum(low.astype(BF16), "tensor")
    delta = jnp.einsum("tnr,trd->tnd", low, tile_up, preferred_element_type=F32).reshape(n * rows, feat)
    part = jnp.dot(local, w, preferred_element_type=F32).astype(BF16)
    w_own = lax.dynamic_slice_in_dim(w, ti * feat, feat, 1)
    own = jnp.dot(local, w_own, preferred_element_type=F32) + delta
    part = lax.dynamic_update_slice_in_dim(part, own.astype(BF16), ti * feat, 1)
    return lax.psum_scatter(part, "tensor", scatter_dimension=0, tiled=True)


def solution(mesh):
    return jax.shard_map(
        body,
        mesh=mesh,
        in_specs=(
            P(("groups", "store", "tensor"), None),
            P("tensor", None),
            P("store", None, "tensor"),
            P("store", None, "tensor"),
            P("groups"),
            P(),
        ),
        out_specs=P(("groups", "store", "tensor"), None),
        check_vma=False,
    )
```

```python
import jax
import jax.numpy as jnp
from jax import lax
from jax.experimental import pallas as pl
from jax.experimental.pallas import tpu as pltpu
from jax.sharding import PartitionSpec as P

TILE = 128
F32 = jnp.float32
BF16 = jnp.bfloat16


def xor_perm(x, axis, d):
    return lax.ppermute(x, axis, [(i, i ^ d) for i in range(lax.axis_size(axis))])


def pick(bank, first, slots):
    count = bank.shape[0]
    held = (slots >= first) & (slots < first + count)
    return jnp.take(bank, jnp.clip(slots - first, 0, count - 1), axis=0), held[:, None, None]


def fetch_maps(bank, slots, me):
    n = lax.axis_size("store")
    first = me * bank.shape[0]
    if n != 4:
        return jnp.take(lax.all_gather(bank, "store", axis=0, tiled=True), slots[me], axis=0)
    own, own_held = pick(bank, first, slots[me])
    mate, _ = pick(bank, first, slots[me ^ 1])
    far, far_held = pick(bank, first, slots[me ^ 2])
    far_mate, _ = pick(bank, first, slots[me ^ 3])
    from_mate = xor_perm(mate, "store", 1)
    far_from_mate = xor_perm(far_mate, "store", 1)
    from_far = xor_perm(jnp.where(far_held, far, far_from_mate), "store", 2)
    mate_first = (me ^ 1) * bank.shape[0]
    mate_held = (slots[me] >= mate_first) & (slots[me] < mate_first + bank.shape[0])
    return jnp.where(own_held, own, jnp.where(mate_held[:, None, None], from_mate, from_far))


def general_body(x, w, down, up, ids, slot_of):
    stores = lax.axis_size("store")
    n = lax.axis_size("tensor")
    si = lax.axis_index("store")
    ti = lax.axis_index("tensor")
    rows = x.shape[0]
    feat = w.shape[0]
    slots = slot_of[ids.reshape(-1, TILE)[:, 0]].reshape(stores, -1)
    tiles = slots.shape[1]
    blocks = x.reshape(rows, n, feat).transpose(1, 0, 2)
    blocks = lax.all_to_all(blocks, "tensor", split_axis=0, concat_axis=0, tiled=True)
    local = blocks.reshape(n * rows, feat)
    tile_down = fetch_maps(down, slots, si)
    tile_up = fetch_maps(up, slots, si)
    low = jnp.einsum("tnd,trd->tnr", local.reshape(tiles, TILE, feat), tile_down, preferred_element_type=F32)
    low = lax.psum(low.astype(BF16), "tensor")
    delta = jnp.einsum("tnr,trd->tnd", low, tile_up, preferred_element_type=F32).reshape(n * rows, feat)
    part = jnp.dot(local, w, preferred_element_type=F32).astype(BF16)
    w_own = lax.dynamic_slice_in_dim(w, ti * feat, feat, 1)
    own = jnp.dot(local, w_own, preferred_element_type=F32) + delta
    part = lax.dynamic_update_slice_in_dim(part, own.astype(BF16), ti * feat, 1)
    return lax.psum_scatter(part, "tensor", scatter_dimension=0, tiled=True)


PLANE = ("groups", "store")
COLS = 512
VMEM = 48 * 1024 * 1024


def chunk_partial(ti, blocks, feat, width, rows, w, term, terms, d, arrived, whole=None, into=None):
    first, stride = blocks
    count, depth = rows.shape
    per = width // COLS
    step = feat // COLS
    packed = lambda b, k, t: (0, b * per + k)
    spread = lambda b, k, t: (0, (first + b * stride) * step + k)
    operands = [rows, w]
    specs = [pl.BlockSpec((count, depth), lambda b, k, t: (0, 0)), pl.BlockSpec((depth, COLS), spread)]
    if term:
        operands.append(terms)
        specs.append(pl.BlockSpec((None, count, COLS), lambda b, k, t: (d, 0, k)))
    for piece in arrived:
        operands.append(piece)
        specs.append(pl.BlockSpec((count, COLS), packed))
    aliases = {}
    if into is not None:
        aliases = {1 + len(operands): 0}
        operands.append(into)
        specs.append(pl.BlockSpec(memory_space=pl.ANY))

    def kernel(t_ref, rows_ref, w_ref, *refs):
        total = jnp.dot(rows_ref[...], w_ref[...], preferred_element_type=F32)
        refs, out_ref = list(refs[:-1]), refs[-1]
        if term:
            own = first + pl.program_id(0) * stride == t_ref[0]
            total = total + jnp.where(own, refs.pop(0)[...].astype(F32), 0.0)
        for ref in refs[: len(arrived)]:
            total = total + ref[...].astype(F32)
        out_ref[...] = total.astype(BF16)

    out_cols = whole if whole else 2 * width
    return pl.pallas_call(
        kernel,
        grid_spec=pltpu.PrefetchScalarGridSpec(
            num_scalar_prefetch=1,
            grid=(2, per),
            in_specs=specs,
            out_specs=pl.BlockSpec((count, COLS), spread if whole else packed),
        ),
        out_shape=jax.ShapeDtypeStruct((count, out_cols), BF16),
        input_output_aliases=aliases,
        compiler_params=pltpu.CompilerParams(vmem_limit_bytes=VMEM),
        cost_estimate=pl.CostEstimate(
            flops=4 * count * depth * width, bytes_accessed=4 * depth * width + 8 * count * width, transcendentals=0
        ),
    )(ti, *operands)


def plane_product(ti, gathered, shards, total, out_dtype):
    m, _ = gathered.shape
    depth, cols = shards[0][1].shape
    tm = 256
    operands, specs = [], []
    for d, shard in shards:
        operands += [gathered, shard]
        specs += [
            pl.BlockSpec((tm, depth), lambda i, t, d=d: (i, t[0] ^ d)),
            pl.BlockSpec((depth, cols), lambda i, t: (0, 0)),
        ]
    if total is not None:
        operands.append(total)
        specs.append(pl.BlockSpec((tm, cols), lambda i, t: (i, 0)))

    def kernel(t_ref, *refs):
        acc = None
        for at in range(len(shards)):
            term = jnp.dot(refs[2 * at][...], refs[2 * at + 1][...], preferred_element_type=F32)
            acc = term if acc is None else acc + term
        if total is not None:
            acc = acc + refs[-2][...]
        refs[-1][...] = acc.astype(out_dtype)

    return pl.pallas_call(
        kernel,
        grid_spec=pltpu.PrefetchScalarGridSpec(
            num_scalar_prefetch=1,
            grid=(m // tm,),
            in_specs=specs,
            out_specs=pl.BlockSpec((tm, cols), lambda i, t: (i, 0)),
        ),
        out_shape=jax.ShapeDtypeStruct((m, cols), out_dtype),
        compiler_params=pltpu.CompilerParams(vmem_limit_bytes=VMEM),
        cost_estimate=pl.CostEstimate(
            flops=2 * m * depth * cols * len(shards),
            bytes_accessed=(2 * m * depth + 2 * depth * cols) * len(shards) + 8 * m * cols,
            transcendentals=0,
        ),
    )(ti, *operands)


def plane_finish(ti, back, low, up_rel, feat, width, into):
    parts, count, cols = back.shape
    per = (feat - width) // cols
    tiles, tile, rank = low.shape

    def kernel(t_ref, back_ref, low_ref, up_ref, into_ref, out_ref):
        for t in range(tiles):
            delta = jnp.dot(low_ref[t], up_ref[t], preferred_element_type=F32).astype(BF16)
            at = pl.ds(t * tile, tile)
            out_ref[at, :] = (back_ref[at, :].astype(F32) + delta.astype(F32)).astype(BF16)

    return pl.pallas_call(
        kernel,
        grid_spec=pltpu.PrefetchScalarGridSpec(
            num_scalar_prefetch=1,
            grid=(parts // per, per),
            in_specs=[
                pl.BlockSpec((None, count, cols), lambda j, k, t: (j * per + k, 0, 0)),
                pl.BlockSpec((tiles, tile, rank), lambda j, k, t: (0, 0, 0)),
                pl.BlockSpec((None, tiles, rank, cols), lambda j, k, t: (j ^ t[0], 0, 0, k)),
                pl.BlockSpec(memory_space=pl.ANY),
            ],
            out_specs=pl.BlockSpec((count, cols), lambda j, k, t: (0, j * (feat // cols) + width // cols + k)),
        ),
        out_shape=jax.ShapeDtypeStruct(into.shape, BF16),
        input_output_aliases={4: 0},
        compiler_params=pltpu.CompilerParams(vmem_limit_bytes=VMEM),
        cost_estimate=pl.CostEstimate(
            flops=2 * parts * count * cols * rank, bytes_accessed=5 * parts * count * cols, transcendentals=0
        ),
    )(ti, back, low, up_rel, into)


SPLIT = 2


def line_body(x, w, down, up, ids, slot_of):
    stores = lax.axis_size("store")
    members = lax.axis_size("groups") * stores
    n = 4
    si = lax.axis_index("store")
    ti = lax.axis_index("tensor")
    pi = lax.axis_index("groups") * stores + si
    scalar = ti.astype(jnp.int32).reshape(1)
    rows = x.shape[0]
    feat = w.shape[0]
    own_tiles = rows // TILE
    rank = down.shape[1]
    plane_width = feat // SPLIT
    width = feat - plane_width
    end = (ti == 0) | (ti == n - 1)
    ends_out = [(0, 1), (3, 2)]
    inward_right, inward_left = [(0, 1), (1, 2)], [(3, 2), (2, 1)]
    middle = [(1, 2), (2, 1)]
    to_ends = [(1, 0), (2, 3)]
    send = lambda v, pairs: lax.ppermute(v, "tensor", pairs)

    slots = slot_of[ids.reshape(-1, TILE)[:, 0]].reshape(stores, n, own_tiles)
    slots = jnp.take(slots, ti ^ jnp.arange(n), axis=1).reshape(stores, n * own_tiles)

    piece = [lax.dynamic_slice_in_dim(x, (ti ^ d) * feat, feat, 1) for d in range(n)]
    for d in (3, 2, 1):
        piece[d] = xor_perm(piece[d], "tensor", d)

    gathered = lax.all_gather(x, PLANE, axis=0, tiled=True)
    tile_down = fetch_maps(down, slots, si)
    tile_up = fetch_maps(up, slots, si)

    cols = plane_width * n // members
    per = plane_width // cols
    w_own = lax.dynamic_slice_in_dim(w, (pi // per) * feat + width + (pi % per) * cols, cols, 1)
    w_own, piece[1], piece[2], piece[3] = lax.optimization_barrier((w_own, piece[1], piece[2], piece[3]))
    w_near = xor_perm(w_own, "tensor", 1)
    w_mid = send(w_own, middle)
    w_end2 = send(w_mid, to_ends)
    w_mid2 = send(w_near, middle)
    w_end3 = send(w_mid2, to_ends)
    w_two = jnp.where(end, w_end2, w_mid2)
    w_three = jnp.where(end, w_end3, w_mid)

    low = jnp.stack([
        jnp.einsum(
            "tnd,trd->tnr",
            piece[d].reshape(own_tiles, TILE, feat),
            tile_down[d * own_tiles : (d + 1) * own_tiles],
            preferred_element_type=F32,
        )
        for d in range(n)
    ])
    pair = low.shape[1:]
    near = xor_perm(low.astype(BF16), "tensor", 1).reshape(2, 2, *pair)[:, ::-1].reshape(n, *pair)
    low = low + near.astype(F32)
    far = xor_perm(low.astype(BF16), "tensor", 2).reshape(2, 2, *pair)[::-1].reshape(n, *pair)
    low = (low + far.astype(F32)).astype(BF16)
    tile_up = tile_up.reshape(n, own_tiles, rank, feat)
    terms = jnp.einsum("dtnr,dtrc->dtnc", low, tile_up[..., :width], preferred_element_type=F32)
    terms = terms.astype(BF16).reshape(n, rows, width)
    up_plane = tile_up[..., width:]
    up_rel = jnp.stack([up_plane[0]] + [xor_perm(up_plane[d], "tensor", d) for d in range(1, n)])

    def partial(chunk, d, arrived=(), term=True, **kw):
        return chunk_partial(scalar, chunk, feat, width, piece[d], w, term, terms, d, arrived, **kw)

    inner, outer = (1, 1), (0, 3)
    first = [send(partial(inner, 3, term=False), ends_out), send(partial(outer, 3), ends_out)]
    out = None
    arrived = []
    for chunk, came in zip((inner, outer), first):
        second = partial(chunk, 2, (came,))
        right, left = send(second, inward_right), send(second, inward_left)
        to_near = partial(chunk, 1, (jnp.where(ti == 1, left, right),))
        to_mid = partial(chunk, 3, (jnp.where(ti == 1, right, left),))
        arrived.append((xor_perm(to_near, "tensor", 1), send(to_mid, middle)))

    total = plane_product(scalar, gathered, [(0, w_own), (1, w_near)], None, F32)
    total = plane_product(scalar, gathered, [(2, w_two), (3, w_three)], total, BF16)
    back = lax.all_to_all(total.reshape(members, rows, cols), PLANE, split_axis=0, concat_axis=0, tiled=True)

    for chunk, came in zip((inner, outer), arrived):
        out = partial(chunk, 0, came, whole=n * feat, into=out)
    return plane_finish(scalar, back, low[0], up_rel, feat, width, out)


def body(x, w, down, up, ids, slot_of):
    line = lax.axis_size("tensor") == 4 and lax.axis_size("store") == 4 and lax.axis_size("groups") == 2
    line = line and x.shape[0] % TILE == 0 and w.shape[0] % (2 * COLS) == 0
    return (line_body if line else general_body)(x, w, down, up, ids, slot_of)


def solution(mesh):
    return jax.shard_map(
        body,
        mesh=mesh,
        in_specs=(
            P(("groups", "store", "tensor"), None),
            P("tensor", None),
            P("store", None, "tensor"),
            P("store", None, "tensor"),
            P("groups"),
            P(),
        ),
        out_specs=P(("groups", "store", "tensor"), None),
        check_vma=False,
    )
```

```python
import jax
import jax.numpy as jnp
from jax import lax
from jax.experimental import pallas as pl
from jax.experimental.pallas import tpu as pltpu
from jax.sharding import PartitionSpec as P

TILE = 128
F32 = jnp.float32
BF16 = jnp.bfloat16


def xor_perm(x, axis, d):
    return lax.ppermute(x, axis, [(i, i ^ d) for i in range(lax.axis_size(axis))])


def pick(bank, first, slots):
    count = bank.shape[0]
    held = (slots >= first) & (slots < first + count)
    return jnp.take(bank, jnp.clip(slots - first, 0, count - 1), axis=0), held[:, None, None]


def fetch_maps(bank, slots, me):
    n = lax.axis_size("store")
    first = me * bank.shape[0]
    if n != 4:
        return jnp.take(lax.all_gather(bank, "store", axis=0, tiled=True), slots[me], axis=0)
    own, own_held = pick(bank, first, slots[me])
    mate, _ = pick(bank, first, slots[me ^ 1])
    far, far_held = pick(bank, first, slots[me ^ 2])
    far_mate, _ = pick(bank, first, slots[me ^ 3])
    from_mate = xor_perm(mate, "store", 1)
    far_from_mate = xor_perm(far_mate, "store", 1)
    from_far = xor_perm(jnp.where(far_held, far, far_from_mate), "store", 2)
    mate_first = (me ^ 1) * bank.shape[0]
    mate_held = (slots[me] >= mate_first) & (slots[me] < mate_first + bank.shape[0])
    return jnp.where(own_held, own, jnp.where(mate_held[:, None, None], from_mate, from_far))


def general_body(x, w, down, up, ids, slot_of):
    stores = lax.axis_size("store")
    n = lax.axis_size("tensor")
    si = lax.axis_index("store")
    ti = lax.axis_index("tensor")
    rows = x.shape[0]
    feat = w.shape[0]
    slots = slot_of[ids.reshape(-1, TILE)[:, 0]].reshape(stores, -1)
    tiles = slots.shape[1]
    blocks = x.reshape(rows, n, feat).transpose(1, 0, 2)
    blocks = lax.all_to_all(blocks, "tensor", split_axis=0, concat_axis=0, tiled=True)
    local = blocks.reshape(n * rows, feat)
    tile_down = fetch_maps(down, slots, si)
    tile_up = fetch_maps(up, slots, si)
    low = jnp.einsum("tnd,trd->tnr", local.reshape(tiles, TILE, feat), tile_down, preferred_element_type=F32)
    low = lax.psum(low.astype(BF16), "tensor")
    delta = jnp.einsum("tnr,trd->tnd", low, tile_up, preferred_element_type=F32).reshape(n * rows, feat)
    part = jnp.dot(local, w, preferred_element_type=F32).astype(BF16)
    w_own = lax.dynamic_slice_in_dim(w, ti * feat, feat, 1)
    own = jnp.dot(local, w_own, preferred_element_type=F32) + delta
    part = lax.dynamic_update_slice_in_dim(part, own.astype(BF16), ti * feat, 1)
    return lax.psum_scatter(part, "tensor", scatter_dimension=0, tiled=True)


PLANE = ("groups", "store")
COLS = 512
VMEM = 48 * 1024 * 1024


def chunk_partial(ti, blocks, feat, width, rows, w, term, terms, d, arrived, whole=None, into=None):
    first, stride = blocks
    _, count, depth = rows.shape
    per = width // COLS
    step = feat // COLS
    packed = lambda b, k, t: (0, b * per + k)
    spread = lambda b, k, t: (0, (first + b * stride) * step + k)
    operands = [rows, w]
    specs = [pl.BlockSpec((None, count, depth), lambda b, k, t: (t[0] ^ d, 0, 0)), pl.BlockSpec((depth, COLS), spread)]
    if term:
        operands.append(terms)
        specs.append(pl.BlockSpec((None, count, COLS), lambda b, k, t: (t[0] ^ d, 0, k)))
    for piece in arrived:
        operands.append(piece)
        specs.append(pl.BlockSpec((count, COLS), packed))
    aliases = {}
    if into is not None:
        aliases = {1 + len(operands): 0}
        operands.append(into)
        specs.append(pl.BlockSpec(memory_space=pl.ANY))

    def kernel(t_ref, rows_ref, w_ref, *refs):
        total = jnp.dot(rows_ref[...], w_ref[...], preferred_element_type=F32)
        refs, out_ref = list(refs[:-1]), refs[-1]
        if term:
            own = first + pl.program_id(0) * stride == t_ref[0]
            total = total + jnp.where(own, refs.pop(0)[...].astype(F32), 0.0)
        for ref in refs[: len(arrived)]:
            total = total + ref[...].astype(F32)
        out_ref[...] = total.astype(BF16)

    out_cols = whole if whole else 2 * width
    return pl.pallas_call(
        kernel,
        grid_spec=pltpu.PrefetchScalarGridSpec(
            num_scalar_prefetch=1,
            grid=(2, per),
            in_specs=specs,
            out_specs=pl.BlockSpec((count, COLS), spread if whole else packed),
        ),
        out_shape=jax.ShapeDtypeStruct((count, out_cols), BF16),
        input_output_aliases=aliases,
        compiler_params=pltpu.CompilerParams(vmem_limit_bytes=VMEM),
        cost_estimate=pl.CostEstimate(
            flops=4 * count * depth * width, bytes_accessed=4 * depth * width + 8 * count * width, transcendentals=0
        ),
    )(ti, *operands)


def plane_product(ti, gathered, shards):
    m, _ = gathered.shape
    depth, cols = shards[0][1].shape
    tm = 256
    operands, specs = [], []
    for d, shard in shards:
        operands += [gathered, shard]
        specs += [
            pl.BlockSpec((tm, depth), lambda i, t, d=d: (i, t[0] ^ d)),
            pl.BlockSpec((depth, cols), lambda i, t: (0, 0)),
        ]

    def kernel(t_ref, *refs):
        acc = jnp.zeros((tm, cols), F32)
        for at in range(len(shards)):
            acc = acc + jnp.dot(refs[2 * at][...], refs[2 * at + 1][...], preferred_element_type=F32)
        refs[-1][...] = acc.astype(BF16)

    return pl.pallas_call(
        kernel,
        grid_spec=pltpu.PrefetchScalarGridSpec(
            num_scalar_prefetch=1,
            grid=(m // tm,),
            in_specs=specs,
            out_specs=pl.BlockSpec((tm, cols), lambda i, t: (i, 0)),
        ),
        out_shape=jax.ShapeDtypeStruct((m, cols), BF16),
        compiler_params=pltpu.CompilerParams(vmem_limit_bytes=VMEM),
        cost_estimate=pl.CostEstimate(
            flops=2 * m * depth * cols * len(shards),
            bytes_accessed=(2 * m * depth + 2 * depth * cols) * len(shards) + 2 * m * cols,
            transcendentals=0,
        ),
    )(ti, *operands)


def plane_finish(ti, back, low, up_plane, feat, width, into, h):
    parts, tile, cols = back.shape
    per = (feat - width) // cols
    rank = low.shape[-1]

    def kernel(t_ref, back_ref, low_ref, up_ref, into_ref, out_ref):
        delta = jnp.dot(low_ref[...], up_ref[...], preferred_element_type=F32).astype(BF16)
        out_ref[...] = (back_ref[...].astype(F32) + delta.astype(F32)).astype(BF16)

    return pl.pallas_call(
        kernel,
        grid_spec=pltpu.PrefetchScalarGridSpec(
            num_scalar_prefetch=1,
            grid=(parts // per, per),
            in_specs=[
                pl.BlockSpec((None, tile, cols), lambda j, k, t: (j * per + k, 0, 0)),
                pl.BlockSpec((None, None, tile, rank), lambda j, k, t: (t[0], h, 0, 0)),
                pl.BlockSpec((None, None, rank, cols), lambda j, k, t: (j, h, 0, k)),
                pl.BlockSpec(memory_space=pl.ANY),
            ],
            out_specs=pl.BlockSpec((tile, cols), lambda j, k, t: (h, j * (feat // cols) + width // cols + k)),
        ),
        out_shape=jax.ShapeDtypeStruct(into.shape, BF16),
        input_output_aliases={4: 0},
        compiler_params=pltpu.CompilerParams(vmem_limit_bytes=VMEM),
        cost_estimate=pl.CostEstimate(
            flops=2 * parts * tile * cols * rank, bytes_accessed=5 * parts * tile * cols, transcendentals=0
        ),
    )(ti, back, low, up_plane, into)


def tile_slot(t, i, place):
    ids, slot_of, meta = t
    last = ids.shape[0] // TILE - 1
    return slot_of[ids[jnp.minimum(place * meta[2] + i, last) * TILE]]


def held_index(t, slot, count):
    return jnp.clip(slot - t[2][0] * count, 0, count - 1)


def map_call(kernel, scalars, grid, in_specs, out_specs, out_shape, nbytes, flops=0):
    return pl.pallas_call(
        kernel,
        grid_spec=pltpu.PrefetchScalarGridSpec(
            num_scalar_prefetch=3, grid=grid, in_specs=in_specs, out_specs=out_specs
        ),
        out_shape=out_shape,
        compiler_params=pltpu.CompilerParams(vmem_limit_bytes=VMEM),
        cost_estimate=pl.CostEstimate(flops=flops, bytes_accessed=nbytes, transcendentals=0),
    )


def maps_for_mate(scalars, bank, tiles, rows=None):
    count, rank, feat = bank.shape
    steps = 2 * tiles

    def at(h, i, *t):
        return (held_index(t, tile_slot(t, i, t[2][0] ^ (1 + 2 * h)), count), 0, 0)

    tile = lambda h, i, *t: (h * tiles + i, 0, 0)
    in_specs = [pl.BlockSpec((1, rank, feat), at)]
    out_specs = [pl.BlockSpec((1, rank, feat), tile)]
    out_shape = [jax.ShapeDtypeStruct((steps, rank, feat), BF16)]
    operands = [bank]
    if rows is not None:
        n = rows.shape[1] // feat
        some = rows.shape[0] // steps
        in_specs.append(pl.BlockSpec((some, n * feat), lambda h, i, *t: (h * tiles + i, 0)))
        out_specs.append(pl.BlockSpec((n, some, feat), lambda h, i, *t: (0, h * tiles + i, 0)))
        out_shape.append(jax.ShapeDtypeStruct((n, rows.shape[0], feat), BF16))
        operands.append(rows)

    def kernel(ids, slot_of, meta, bank_ref, *refs):
        if rows is None:
            refs[0][...] = bank_ref[...]
        else:
            rows_ref, out_ref, blocks_ref = refs
            out_ref[...] = bank_ref[...]
            for j in range(n):
                blocks_ref[j] = rows_ref[:, j * feat : (j + 1) * feat]

    return map_call(
        kernel, scalars, (2, tiles), in_specs, out_specs, out_shape, 4 * steps * rank * feat
    )(*scalars, *operands)


def maps_for_far(scalars, bank, got, tiles):
    count, rank, feat = bank.shape

    def at(i, *t):
        return (held_index(t, tile_slot(t, i, t[2][0] ^ 2), count), 0, 0)

    def kernel(ids, slot_of, meta, bank_ref, got_ref, out_ref):
        slot = tile_slot((ids, slot_of, meta), pl.program_id(0), meta[0] ^ 2)
        mine = slot // count == meta[0]

        @pl.when(mine)
        def _():
            out_ref[...] = bank_ref[...]

        @pl.when(jnp.logical_not(mine))
        def _():
            out_ref[...] = got_ref[...]

    return map_call(
        kernel, scalars, (tiles,),
        [pl.BlockSpec((1, rank, feat), at), pl.BlockSpec((1, rank, feat), lambda i, *t: (tiles + i, 0, 0))],
        pl.BlockSpec((1, rank, feat), lambda i, *t: (i, 0, 0)),
        jax.ShapeDtypeStruct((tiles, rank, feat), BF16),
        6 * tiles * rank * feat,
    )(*scalars, bank, got)


def own_specs(bank, tiles):
    count, rank, feat = bank.shape

    def at(i, *t):
        return (held_index(t, tile_slot(t, i, t[2][0]), count), 0, 0)

    tile = lambda i, *t: (i, 0, 0)
    block = (None, rank, feat)
    return [pl.BlockSpec(block, at), pl.BlockSpec(block, tile), pl.BlockSpec(block, tile)]


def with_own(scalar_refs, count, refs, use):
    meta = scalar_refs[2]
    place = tile_slot(scalar_refs, pl.program_id(0), meta[0]) // count
    here, mate = place == meta[0], place == (meta[0] ^ 1)
    far = jnp.logical_not(jnp.logical_or(here, mate))
    for flag, ref in zip((here, mate, far), refs):
        pl.when(flag)(lambda ref=ref: use(ref))


def low_parts(scalars, rows, bank, got, far, tiles):
    count, rank, feat = bank.shape

    def kernel(ids, slot_of, meta, rows_ref, bank_ref, got_ref, far_ref, out_ref):
        def use(ref):
            out_ref[...] = lax.dot_general(
                rows_ref[...], ref[...], (((1,), (1,)), ((), ())), preferred_element_type=F32
            )

        with_own((ids, slot_of, meta), count, (bank_ref, got_ref, far_ref), use)

    return map_call(
        kernel, scalars, (tiles,),
        [pl.BlockSpec((None, TILE, feat), lambda i, *t: (i, 0, 0))] + own_specs(bank, tiles),
        pl.BlockSpec((None, TILE, rank), lambda i, *t: (i, 0, 0)),
        jax.ShapeDtypeStruct((tiles, TILE, rank), F32),
        (6 * rank + 2 * TILE) * tiles * feat, 2 * tiles * TILE * rank * feat,
    )(*scalars, rows, bank, got, far)


def adapter_terms(scalars, low, bank, got, far, tiles, width):
    count, rank, feat = bank.shape

    def kernel(ids, slot_of, meta, low_ref, bank_ref, got_ref, far_ref, term_ref, up_ref):
        def use(ref):
            term_ref[...] = jnp.dot(low_ref[...], ref[:, :width], preferred_element_type=F32).astype(BF16)
            up_ref[...] = ref[:, width:]

        with_own((ids, slot_of, meta), count, (bank_ref, got_ref, far_ref), use)

    tile = lambda i, *t: (i, 0, 0)
    return map_call(
        kernel, scalars, (tiles,),
        [pl.BlockSpec((None, TILE, rank), tile)] + own_specs(bank, tiles),
        [pl.BlockSpec((None, TILE, width), tile), pl.BlockSpec((None, rank, feat - width), tile)],
        [
            jax.ShapeDtypeStruct((tiles, TILE, width), BF16),
            jax.ShapeDtypeStruct((tiles, rank, feat - width), BF16),
        ],
        (7 * rank + TILE) * tiles * feat, 2 * tiles * TILE * rank * width,
    )(*scalars, low, bank, got, far)


SPLIT = 2


def line_body(x, w, down, up, ids, slot_of):
    stores = lax.axis_size("store")
    members = lax.axis_size("groups") * stores
    n = 4
    si = lax.axis_index("store")
    ti = lax.axis_index("tensor")
    pi = lax.axis_index("groups") * stores + si
    scalar = ti.astype(jnp.int32).reshape(1)
    rows = x.shape[0]
    feat = w.shape[0]
    own_tiles = rows // TILE
    tiles = n * own_tiles
    rank = down.shape[1]
    plane_width = feat // SPLIT
    width = feat - plane_width
    end = (ti == 0) | (ti == n - 1)
    ends_out = [(0, 1), (3, 2)]
    inward_right, inward_left = [(0, 1), (1, 2)], [(3, 2), (2, 1)]
    middle = [(1, 2), (2, 1)]
    to_ends = [(1, 0), (2, 3)]
    send = lambda v, pairs: lax.ppermute(v, "tensor", pairs)

    meta = jnp.stack([si, ti, jnp.int32(tiles)]).astype(jnp.int32)
    scalars = (ids, slot_of, meta)
    after = lambda value, *others: lax.optimization_barrier((value, *others))[0]

    down_send, blocks = maps_for_mate(scalars, down, tiles, x)
    blocks = lax.all_to_all(blocks, "tensor", split_axis=0, concat_axis=0, tiled=True)
    down_got = xor_perm(down_send, "store", 1)
    down_to_far = maps_for_far(scalars, down, down_got, tiles)
    down_far = xor_perm(down_to_far, "store", 2)
    (up_send,) = maps_for_mate(scalars, up, tiles)
    up_got = xor_perm(up_send, "store", 1)
    up_far = xor_perm(maps_for_far(scalars, up, up_got, tiles), "store", 2)

    cols = plane_width * n // members
    per = plane_width // cols
    w_own = lax.dynamic_slice_in_dim(w, (pi // per) * feat + width + (pi % per) * cols, cols, 1)
    w_near = xor_perm(w_own, "tensor", 1)
    w_mid = send(w_own, middle)

    gathered = []
    for h in range(own_tiles):
        half = after(x[h * TILE : (h + 1) * TILE], up_far, down_far, blocks, w_near, w_mid)
        gathered.append(lax.all_gather(half, PLANE, axis=0, tiled=True))

    low = low_parts(scalars, after(blocks, w_near, w_mid).reshape(tiles, TILE, feat), down, down_got, down_far, tiles)
    low = low + xor_perm(low.astype(BF16), "tensor", 1).astype(F32)
    low = (low + xor_perm(low.astype(BF16), "tensor", 2).astype(F32)).astype(BF16)
    near_on, mid_on = lax.optimization_barrier((w_near, w_mid, low))[:2]
    w_end2 = send(mid_on, to_ends)
    w_mid2 = send(near_on, middle)
    w_end3 = send(w_mid2, to_ends)
    w_two = jnp.where(end, w_end2, w_mid2)
    w_three = jnp.where(end, w_end3, w_mid)
    terms, up_plane = adapter_terms(scalars, low, up, up_got, up_far, tiles, width)
    terms = terms.reshape(n, rows, width)
    up_plane = lax.all_to_all(
        up_plane.reshape(n, own_tiles, rank, plane_width), "tensor", split_axis=0, concat_axis=0, tiled=True
    )

    def partial(chunk, d, arrived=(), term=True, **kw):
        return chunk_partial(scalar, chunk, feat, width, blocks, w, term, terms, d, arrived, **kw)

    inner, outer = (1, 1), (0, 3)
    first = [send(partial(inner, 3, term=False), ends_out), send(partial(outer, 3), ends_out)]
    arrived, seconds = [], []
    for chunk, came in zip((inner, outer), first):
        second = partial(chunk, 2, (came,))
        right, left = send(second, inward_right), send(second, inward_left)
        to_near = partial(chunk, 1, (jnp.where(ti == 1, left, right),))
        to_mid = partial(chunk, 3, (jnp.where(ti == 1, right, left),))
        seconds.append(second)
        arrived.append((xor_perm(to_near, "tensor", 1), send(to_mid, middle)))

    shards = [(0, w_own), (1, w_near), (2, w_two), (3, w_three)]
    waits = [(seconds[1],), arrived[0]]
    back = []
    for h in range(own_tiles):
        total = plane_product(scalar, after(gathered[h], *waits[min(h, 1)]), shards)
        back.append(lax.all_to_all(total.reshape(members, TILE, cols), PLANE, split_axis=0, concat_axis=0, tiled=True))

    out = partial(inner, 0, arrived[0], whole=n * feat)
    low = low.reshape(n, own_tiles, TILE, rank)
    for h in range(own_tiles - 1):
        out = plane_finish(scalar, back[h], low, up_plane, feat, width, out, h)
    out = partial(outer, 0, arrived[1], whole=n * feat, into=out)
    return plane_finish(scalar, back[-1], low, up_plane, feat, width, out, own_tiles - 1)


def body(x, w, down, up, ids, slot_of):
    line = lax.axis_size("tensor") == 4 and lax.axis_size("store") == 4 and lax.axis_size("groups") == 2
    line = line and x.shape[0] % TILE == 0 and w.shape[0] % (2 * COLS) == 0
    return (line_body if line else general_body)(x, w, down, up, ids, slot_of)


def solution(mesh):
    return jax.shard_map(
        body,
        mesh=mesh,
        in_specs=(
            P(("groups", "store", "tensor"), None),
            P("tensor", None),
            P("store", None, "tensor"),
            P("store", None, "tensor"),
            P("groups"),
            P(),
        ),
        out_specs=P(("groups", "store", "tensor"), None),
        check_vma=False,
    )
```

```python
import jax
import jax.numpy as jnp
from jax import lax
from jax.experimental import pallas as pl
from jax.experimental.pallas import tpu as pltpu
from jax.sharding import PartitionSpec as P

TILE = 128
F32 = jnp.float32
BF16 = jnp.bfloat16


def xor_perm(x, axis, d):
    return lax.ppermute(x, axis, [(i, i ^ d) for i in range(lax.axis_size(axis))])


def pick(bank, first, slots):
    count = bank.shape[0]
    held = (slots >= first) & (slots < first + count)
    return jnp.take(bank, jnp.clip(slots - first, 0, count - 1), axis=0), held[:, None, None]


def fetch_maps(bank, slots, me):
    n = lax.axis_size("store")
    first = me * bank.shape[0]
    if n != 4:
        return jnp.take(lax.all_gather(bank, "store", axis=0, tiled=True), slots[me], axis=0)
    own, own_held = pick(bank, first, slots[me])
    mate, _ = pick(bank, first, slots[me ^ 1])
    far, far_held = pick(bank, first, slots[me ^ 2])
    far_mate, _ = pick(bank, first, slots[me ^ 3])
    from_mate = xor_perm(mate, "store", 1)
    far_from_mate = xor_perm(far_mate, "store", 1)
    from_far = xor_perm(jnp.where(far_held, far, far_from_mate), "store", 2)
    mate_first = (me ^ 1) * bank.shape[0]
    mate_held = (slots[me] >= mate_first) & (slots[me] < mate_first + bank.shape[0])
    return jnp.where(own_held, own, jnp.where(mate_held[:, None, None], from_mate, from_far))


def general_body(x, w, down, up, ids, slot_of):
    stores = lax.axis_size("store")
    n = lax.axis_size("tensor")
    si = lax.axis_index("store")
    ti = lax.axis_index("tensor")
    rows = x.shape[0]
    feat = w.shape[0]
    slots = slot_of[ids.reshape(-1, TILE)[:, 0]].reshape(stores, -1)
    tiles = slots.shape[1]
    blocks = x.reshape(rows, n, feat).transpose(1, 0, 2)
    blocks = lax.all_to_all(blocks, "tensor", split_axis=0, concat_axis=0, tiled=True)
    local = blocks.reshape(n * rows, feat)
    tile_down = fetch_maps(down, slots, si)
    tile_up = fetch_maps(up, slots, si)
    low = jnp.einsum("tnd,trd->tnr", local.reshape(tiles, TILE, feat), tile_down, preferred_element_type=F32)
    low = lax.psum(low.astype(BF16), "tensor")
    delta = jnp.einsum("tnr,trd->tnd", low, tile_up, preferred_element_type=F32).reshape(n * rows, feat)
    part = jnp.dot(local, w, preferred_element_type=F32).astype(BF16)
    w_own = lax.dynamic_slice_in_dim(w, ti * feat, feat, 1)
    own = jnp.dot(local, w_own, preferred_element_type=F32) + delta
    part = lax.dynamic_update_slice_in_dim(part, own.astype(BF16), ti * feat, 1)
    return lax.psum_scatter(part, "tensor", scatter_dimension=0, tiled=True)


PLANE = ("groups", "store")
COLS = 512
VMEM = 48 * 1024 * 1024


def chunk_partial(ti, blocks, feat, width, rows, w, term, terms, d, arrived, whole=None, into=None, choose=None, half=None, came_half=0):
    first, stride = blocks
    _, count, depth = rows.shape
    per = width // COLS
    step = feat // COLS
    packed = lambda b, k, t: (0, ((half or 0) * 2 + b) * per + k)
    came = lambda b, k, t: (0, (came_half * 2 + b) * per + k)
    spread = lambda b, k, t: (0, (first + b * stride) * step + k)
    operands = [rows, w]
    specs = [pl.BlockSpec((None, count, depth), lambda b, k, t: (t[0] ^ d, 0, 0)), pl.BlockSpec((depth, COLS), spread)]
    if term:
        operands.append(terms)
        specs.append(pl.BlockSpec((None, count, COLS), lambda b, k, t: (t[0] ^ d, 0, k)))
    for piece in arrived:
        operands.append(piece)
        specs.append(pl.BlockSpec((count, COLS), came))
    aliases = {}
    if into is not None:
        aliases = {1 + len(operands): 0}
        operands.append(into)
        specs.append(pl.BlockSpec(memory_space=pl.ANY))

    def kernel(t_ref, rows_ref, w_ref, *refs):
        total = jnp.dot(rows_ref[...], w_ref[...], preferred_element_type=F32)
        refs, out_ref = list(refs[:-1]), refs[-1]
        if term:
            own = first + pl.program_id(0) * stride == t_ref[0]
            total = total + jnp.where(own, refs.pop(0)[...].astype(F32), 0.0)
        if choose is None:
            for ref in refs[: len(arrived)]:
                total = total + ref[...].astype(F32)
        else:
            one, other = refs[0][...].astype(F32), refs[1][...].astype(F32)
            total = total + jnp.where(t_ref[0] == choose, one, other)
        out_ref[...] = total.astype(BF16)

    out_cols = whole if whole else (2 if half is None else 4) * width
    return pl.pallas_call(
        kernel,
        grid_spec=pltpu.PrefetchScalarGridSpec(
            num_scalar_prefetch=1,
            grid=(2, per),
            in_specs=specs,
            out_specs=pl.BlockSpec((count, COLS), spread if whole else packed),
        ),
        out_shape=jax.ShapeDtypeStruct((count, out_cols), BF16),
        input_output_aliases=aliases,
        compiler_params=pltpu.CompilerParams(vmem_limit_bytes=VMEM),
        cost_estimate=pl.CostEstimate(
            flops=4 * count * depth * width, bytes_accessed=4 * depth * width + 8 * count * width, transcendentals=0
        ),
    )(ti, *operands)


def plane_product(ti, gathered, shards):
    m, _ = gathered.shape
    depth, cols = shards[0][1].shape
    tm = 256
    operands, specs = [], []
    for d, shard in shards:
        operands += [gathered, shard]
        specs += [
            pl.BlockSpec((tm, depth), lambda i, t, d=d: (i, t[0] ^ d)),
            pl.BlockSpec((depth, cols), lambda i, t: (0, 0)),
        ]

    def kernel(t_ref, *refs):
        acc = jnp.zeros((tm, cols), F32)
        for at in range(len(shards)):
            acc = acc + jnp.dot(refs[2 * at][...], refs[2 * at + 1][...], preferred_element_type=F32)
        refs[-1][...] = acc.astype(BF16)

    return pl.pallas_call(
        kernel,
        grid_spec=pltpu.PrefetchScalarGridSpec(
            num_scalar_prefetch=1,
            grid=(m // tm,),
            in_specs=specs,
            out_specs=pl.BlockSpec((tm, cols), lambda i, t: (i, 0)),
        ),
        out_shape=jax.ShapeDtypeStruct((m, cols), BF16),
        compiler_params=pltpu.CompilerParams(vmem_limit_bytes=VMEM),
        cost_estimate=pl.CostEstimate(
            flops=2 * m * depth * cols * len(shards),
            bytes_accessed=(2 * m * depth + 2 * depth * cols) * len(shards) + 2 * m * cols,
            transcendentals=0,
        ),
    )(ti, *operands)


def plane_finish(ti, back, low, up_plane, feat, width, into, h):
    parts, tile, cols = back.shape
    per = (feat - width) // cols
    rank = low.shape[-1]

    def kernel(t_ref, back_ref, low_ref, up_ref, into_ref, out_ref):
        delta = jnp.dot(low_ref[...], up_ref[...], preferred_element_type=F32).astype(BF16)
        out_ref[...] = (back_ref[...].astype(F32) + delta.astype(F32)).astype(BF16)

    return pl.pallas_call(
        kernel,
        grid_spec=pltpu.PrefetchScalarGridSpec(
            num_scalar_prefetch=1,
            grid=(parts // per, per),
            in_specs=[
                pl.BlockSpec((None, tile, cols), lambda j, k, t: (j * per + k, 0, 0)),
                pl.BlockSpec((None, None, tile, rank), lambda j, k, t: (t[0], h, 0, 0)),
                pl.BlockSpec((None, None, rank, cols), lambda j, k, t: (j, h, 0, k)),
                pl.BlockSpec(memory_space=pl.ANY),
            ],
            out_specs=pl.BlockSpec((tile, cols), lambda j, k, t: (h, j * (feat // cols) + width // cols + k)),
        ),
        out_shape=jax.ShapeDtypeStruct(into.shape, BF16),
        input_output_aliases={4: 0},
        compiler_params=pltpu.CompilerParams(vmem_limit_bytes=VMEM),
        cost_estimate=pl.CostEstimate(
            flops=2 * parts * tile * cols * rank, bytes_accessed=5 * parts * tile * cols, transcendentals=0
        ),
    )(ti, back, low, up_plane, into)


def tile_slot(t, i, place):
    ids, slot_of, meta = t
    last = ids.shape[0] // TILE - 1
    return slot_of[ids[jnp.minimum(place * meta[2] + i, last) * TILE]]


def held_index(t, slot, count):
    return jnp.clip(slot - t[2][0] * count, 0, count - 1)


def map_call(kernel, scalars, grid, in_specs, out_specs, out_shape, nbytes, flops=0):
    return pl.pallas_call(
        kernel,
        grid_spec=pltpu.PrefetchScalarGridSpec(
            num_scalar_prefetch=3, grid=grid, in_specs=in_specs, out_specs=out_specs
        ),
        out_shape=out_shape,
        compiler_params=pltpu.CompilerParams(vmem_limit_bytes=VMEM),
        cost_estimate=pl.CostEstimate(flops=flops, bytes_accessed=nbytes, transcendentals=0),
    )


def maps_for_mate(scalars, bank, tiles, rows=None):
    count, rank, feat = bank.shape

    def at(h):
        return lambda i, *t: (held_index(t, tile_slot(t, i, t[2][0] ^ (1 + 2 * h)), count), 0, 0)

    in_specs = [pl.BlockSpec((None, rank, feat), at(h)) for h in range(2)]
    out_specs = [pl.BlockSpec((2, None, rank, feat), lambda i, *t: (0, i, 0, 0))]
    out_shape = [jax.ShapeDtypeStruct((2, tiles, rank, feat), BF16)]
    operands = [bank, bank]
    if rows is not None:
        n = rows.shape[1] // feat
        some = rows.shape[0] // tiles
        in_specs.append(pl.BlockSpec((some, n * feat), lambda i, *t: (i, 0)))
        out_specs.append(pl.BlockSpec((n, some, feat), lambda i, *t: (0, i, 0)))
        out_shape.append(jax.ShapeDtypeStruct((n, rows.shape[0], feat), BF16))
        operands.append(rows)

    def kernel(ids, slot_of, meta, one_ref, other_ref, *refs):
        out_ref = refs[0] if rows is None else refs[1]
        out_ref[0] = one_ref[...]
        out_ref[1] = other_ref[...]
        if rows is not None:
            for j in range(n):
                refs[2][j] = refs[0][:, j * feat : (j + 1) * feat]

    out = map_call(
        kernel, scalars, (tiles,), in_specs, out_specs, out_shape, 8 * tiles * rank * feat
    )(*scalars, *operands)
    return [out[0].reshape(2 * tiles, rank, feat)] + list(out[1:])


def maps_for_far(scalars, bank, got, tiles):
    count, rank, feat = bank.shape

    def at(i, *t):
        return (held_index(t, tile_slot(t, i, t[2][0] ^ 2), count), 0, 0)

    def kernel(ids, slot_of, meta, bank_ref, got_ref, out_ref):
        slot = tile_slot((ids, slot_of, meta), pl.program_id(0), meta[0] ^ 2)
        mine = slot // count == meta[0]

        @pl.when(mine)
        def _():
            out_ref[...] = bank_ref[...]

        @pl.when(jnp.logical_not(mine))
        def _():
            out_ref[...] = got_ref[...]

    return map_call(
        kernel, scalars, (tiles,),
        [pl.BlockSpec((1, rank, feat), at), pl.BlockSpec((1, rank, feat), lambda i, *t: (tiles + i, 0, 0))],
        pl.BlockSpec((1, rank, feat), lambda i, *t: (i, 0, 0)),
        jax.ShapeDtypeStruct((tiles, rank, feat), BF16),
        6 * tiles * rank * feat,
    )(*scalars, bank, got)


def own_specs(bank, tiles):
    count, rank, feat = bank.shape

    def at(i, *t):
        return (held_index(t, tile_slot(t, i, t[2][0]), count), 0, 0)

    tile = lambda i, *t: (i, 0, 0)
    block = (None, rank, feat)
    return [pl.BlockSpec(block, at), pl.BlockSpec(block, tile), pl.BlockSpec(block, tile)]


def with_own(scalar_refs, count, refs, use):
    meta = scalar_refs[2]
    place = tile_slot(scalar_refs, pl.program_id(0), meta[0]) // count
    here, mate = place == meta[0], place == (meta[0] ^ 1)
    far = jnp.logical_not(jnp.logical_or(here, mate))
    for flag, ref in zip((here, mate, far), refs):
        pl.when(flag)(lambda ref=ref: use(ref))


def low_parts(scalars, rows, bank, got, far, tiles):
    count, rank, feat = bank.shape

    def kernel(ids, slot_of, meta, rows_ref, bank_ref, got_ref, far_ref, out_ref):
        def use(ref):
            out_ref[...] = lax.dot_general(
                rows_ref[...], ref[...], (((1,), (1,)), ((), ())), preferred_element_type=F32
            )

        with_own((ids, slot_of, meta), count, (bank_ref, got_ref, far_ref), use)

    return map_call(
        kernel, scalars, (tiles,),
        [pl.BlockSpec((None, TILE, feat), lambda i, *t: (i, 0, 0))] + own_specs(bank, tiles),
        pl.BlockSpec((None, TILE, rank), lambda i, *t: (i, 0, 0)),
        jax.ShapeDtypeStruct((tiles, TILE, rank), F32),
        (6 * rank + 2 * TILE) * tiles * feat, 2 * tiles * TILE * rank * feat,
    )(*scalars, rows, bank, got, far)


def adapter_terms(scalars, low, bank, got, far, tiles, width):
    count, rank, feat = bank.shape

    def kernel(ids, slot_of, meta, low_ref, bank_ref, got_ref, far_ref, term_ref, up_ref):
        def use(ref):
            term_ref[...] = jnp.dot(low_ref[...], ref[:, :width], preferred_element_type=F32).astype(BF16)
            up_ref[...] = ref[:, width:]

        with_own((ids, slot_of, meta), count, (bank_ref, got_ref, far_ref), use)

    tile = lambda i, *t: (i, 0, 0)
    return map_call(
        kernel, scalars, (tiles,),
        [pl.BlockSpec((None, TILE, rank), tile)] + own_specs(bank, tiles),
        [pl.BlockSpec((None, TILE, width), tile), pl.BlockSpec((None, rank, feat - width), tile)],
        [
            jax.ShapeDtypeStruct((tiles, TILE, width), BF16),
            jax.ShapeDtypeStruct((tiles, rank, feat - width), BF16),
        ],
        (7 * rank + TILE) * tiles * feat, 2 * tiles * TILE * rank * width,
    )(*scalars, low, bank, got, far)


SPLIT = 2


def line_body(x, w, down, up, ids, slot_of):
    stores = lax.axis_size("store")
    members = lax.axis_size("groups") * stores
    n = 4
    si = lax.axis_index("store")
    ti = lax.axis_index("tensor")
    pi = lax.axis_index("groups") * stores + si
    scalar = ti.astype(jnp.int32).reshape(1)
    rows = x.shape[0]
    feat = w.shape[0]
    own_tiles = rows // TILE
    tiles = n * own_tiles
    rank = down.shape[1]
    plane_width = feat // SPLIT
    width = feat - plane_width
    end = (ti == 0) | (ti == n - 1)
    ends_out = [(0, 1), (3, 2)]
    inward_right, inward_left = [(0, 1), (1, 2)], [(3, 2), (2, 1)]
    middle = [(1, 2), (2, 1)]
    to_ends = [(1, 0), (2, 3)]
    send = lambda v, pairs: lax.ppermute(v, "tensor", pairs)

    meta = jnp.stack([si, ti, jnp.int32(tiles)]).astype(jnp.int32)
    scalars = (ids, slot_of, meta)
    after = lambda value, *others: lax.optimization_barrier((value, *others))[0]

    down_send, blocks = maps_for_mate(scalars, down, tiles, x)
    blocks = lax.all_to_all(blocks, "tensor", split_axis=0, concat_axis=0, tiled=True)
    down_got = xor_perm(down_send, "store", 1)
    down_to_far = maps_for_far(scalars, down, down_got, tiles)
    down_far = xor_perm(down_to_far, "store", 2)
    (up_send,) = maps_for_mate(after(scalars, down_send), up, tiles)
    up_got = xor_perm(up_send, "store", 1)
    up_far = xor_perm(maps_for_far(scalars, up, up_got, tiles), "store", 2)

    cols = plane_width * n // members
    per = plane_width // cols
    w_own = lax.dynamic_slice_in_dim(w, (pi // per) * feat + width + (pi % per) * cols, cols, 1)
    w_near = xor_perm(w_own, "tensor", 1)
    w_mid = send(w_own, middle)

    gathered = []
    for h in range(own_tiles):
        half = after(x[h * TILE : (h + 1) * TILE], up_far, down_far, blocks)
        gathered.append(lax.all_gather(half, PLANE, axis=0, tiled=True))

    low = low_parts(scalars, blocks.reshape(tiles, TILE, feat), down, down_got, down_far, tiles)
    low = low + xor_perm(low.astype(BF16), "tensor", 1).astype(F32)
    low = (low + xor_perm(low.astype(BF16), "tensor", 2).astype(F32)).astype(BF16)
    near_on, mid_on = after(w_near, low), w_mid
    w_end2 = send(mid_on, to_ends)
    w_mid2 = send(near_on, middle)
    terms, up_plane = adapter_terms(scalars, low, up, up_got, up_far, tiles, width)
    terms = terms.reshape(n, rows, width)
    def partial(chunk, d, arrived=(), term=True, **kw):
        return chunk_partial(scalar, chunk, feat, width, blocks, w, term, terms, d, arrived, **kw)

    inner, outer = (1, 1), (0, 3)
    first = [send(partial(inner, 3, term=False), ends_out), send(partial(outer, 3), ends_out)]
    seconds, to_near, to_mid = [], None, None
    for half, (chunk, came) in enumerate(zip((inner, outer), first)):
        second = partial(chunk, 2, (came,))
        seconds.append(second)
        right, left = send(second, inward_right), send(second, inward_left)
        to_near = partial(chunk, 1, (left, right), choose=1, half=half, into=to_near)
        to_mid = partial(chunk, 3, (right, left), choose=1, half=half, into=to_mid)
    lasts = (to_near, to_mid)
    arrived = (xor_perm(to_near, "tensor", 1), send(to_mid, middle))

    w_end3 = send(after(w_mid2, *seconds), to_ends)
    w_two = jnp.where(end, w_end2, w_mid2)
    w_three = jnp.where(end, w_end3, w_mid)
    up_plane = lax.all_to_all(
        up_plane.reshape(n, own_tiles, rank, plane_width), "tensor", split_axis=0, concat_axis=0, tiled=True
    )
    shards = [(0, w_own), (1, w_near), (2, w_two), (3, w_three)]
    waits = [lasts, lasts]
    back = []
    for h in range(own_tiles):
        total = plane_product(scalar, after(gathered[h], *waits[min(h, 1)]), shards)
        back.append(lax.all_to_all(total.reshape(members, TILE, cols), PLANE, split_axis=0, concat_axis=0, tiled=True))

    out = partial(inner, 0, arrived, whole=n * feat, came_half=0)
    low = low.reshape(n, own_tiles, TILE, rank)
    for h in range(own_tiles - 1):
        out = plane_finish(scalar, back[h], low, up_plane, feat, width, out, h)
    out = partial(outer, 0, arrived, whole=n * feat, into=out, came_half=1)
    return plane_finish(scalar, back[-1], low, up_plane, feat, width, out, own_tiles - 1)


def body(x, w, down, up, ids, slot_of):
    line = lax.axis_size("tensor") == 4 and lax.axis_size("store") == 4 and lax.axis_size("groups") == 2
    line = line and x.shape[0] % TILE == 0 and w.shape[0] % (2 * COLS) == 0
    return (line_body if line else general_body)(x, w, down, up, ids, slot_of)


def solution(mesh):
    return jax.shard_map(
        body,
        mesh=mesh,
        in_specs=(
            P(("groups", "store", "tensor"), None),
            P("tensor", None),
            P("store", None, "tensor"),
            P("store", None, "tensor"),
            P("groups"),
            P(),
        ),
        out_specs=P(("groups", "store", "tensor"), None),
        check_vma=False,
    )
```

```python
import jax
import jax.numpy as jnp
from jax import lax
from jax.experimental import pallas as pl
from jax.experimental.pallas import tpu as pltpu
from jax.sharding import PartitionSpec as P

TILE = 128
F32 = jnp.float32
BF16 = jnp.bfloat16


def xor_perm(x, axis, d):
    return lax.ppermute(x, axis, [(i, i ^ d) for i in range(lax.axis_size(axis))])


def pick(bank, first, slots):
    count = bank.shape[0]
    held = (slots >= first) & (slots < first + count)
    return jnp.take(bank, jnp.clip(slots - first, 0, count - 1), axis=0), held[:, None, None]


def fetch_maps(bank, slots, me):
    n = lax.axis_size("store")
    first = me * bank.shape[0]
    if n != 4:
        return jnp.take(lax.all_gather(bank, "store", axis=0, tiled=True), slots[me], axis=0)
    own, own_held = pick(bank, first, slots[me])
    mate, _ = pick(bank, first, slots[me ^ 1])
    far, far_held = pick(bank, first, slots[me ^ 2])
    far_mate, _ = pick(bank, first, slots[me ^ 3])
    from_mate = xor_perm(mate, "store", 1)
    far_from_mate = xor_perm(far_mate, "store", 1)
    from_far = xor_perm(jnp.where(far_held, far, far_from_mate), "store", 2)
    mate_first = (me ^ 1) * bank.shape[0]
    mate_held = (slots[me] >= mate_first) & (slots[me] < mate_first + bank.shape[0])
    return jnp.where(own_held, own, jnp.where(mate_held[:, None, None], from_mate, from_far))


def general_body(x, w, down, up, ids, slot_of):
    stores = lax.axis_size("store")
    n = lax.axis_size("tensor")
    si = lax.axis_index("store")
    ti = lax.axis_index("tensor")
    rows = x.shape[0]
    feat = w.shape[0]
    slots = slot_of[ids.reshape(-1, TILE)[:, 0]].reshape(stores, -1)
    tiles = slots.shape[1]
    blocks = x.reshape(rows, n, feat).transpose(1, 0, 2)
    blocks = lax.all_to_all(blocks, "tensor", split_axis=0, concat_axis=0, tiled=True)
    local = blocks.reshape(n * rows, feat)
    tile_down = fetch_maps(down, slots, si)
    tile_up = fetch_maps(up, slots, si)
    low = jnp.einsum("tnd,trd->tnr", local.reshape(tiles, TILE, feat), tile_down, preferred_element_type=F32)
    low = lax.psum(low.astype(BF16), "tensor")
    delta = jnp.einsum("tnr,trd->tnd", low, tile_up, preferred_element_type=F32).reshape(n * rows, feat)
    part = jnp.dot(local, w, preferred_element_type=F32).astype(BF16)
    w_own = lax.dynamic_slice_in_dim(w, ti * feat, feat, 1)
    own = jnp.dot(local, w_own, preferred_element_type=F32) + delta
    part = lax.dynamic_update_slice_in_dim(part, own.astype(BF16), ti * feat, 1)
    return lax.psum_scatter(part, "tensor", scatter_dimension=0, tiled=True)


PLANE = ("groups", "store")
COLS = 512
VMEM = 48 * 1024 * 1024


def chunk_partial(ti, blocks, feat, width, rows, w, term, terms, d, arrived, whole=None, into=None, choose=None, half=None, dtype=BF16):
    first, stride = blocks
    _, count, depth = rows.shape
    per = width // COLS
    step = feat // COLS
    packed = lambda b, k, t: (0, ((half or 0) * 2 + b) * per + k)
    spread = lambda b, k, t: (0, (first + b * stride) * step + k)
    operands = [rows, w]
    specs = [pl.BlockSpec((None, count, depth), lambda b, k, t: (t[0] ^ d, 0, 0)), pl.BlockSpec((depth, COLS), spread)]
    if term:
        operands.append(terms)
        specs.append(pl.BlockSpec((None, count, COLS), lambda b, k, t: (t[0] ^ d, 0, k)))
    for piece in arrived:
        operands.append(piece)
        specs.append(pl.BlockSpec((count, COLS), lambda b, k, t: (0, b * per + k)))
    aliases = {}
    if into is not None:
        aliases = {1 + len(operands): 0}
        operands.append(into)
        specs.append(pl.BlockSpec(memory_space=pl.ANY))

    def kernel(t_ref, rows_ref, w_ref, *refs):
        total = jnp.dot(rows_ref[...], w_ref[...], preferred_element_type=F32)
        refs, out_ref = list(refs[:-1]), refs[-1]
        if term:
            own = first + pl.program_id(0) * stride == t_ref[0]
            total = total + jnp.where(own, refs.pop(0)[...].astype(F32), 0.0)
        if choose is None:
            for ref in refs[: len(arrived)]:
                total = total + ref[...].astype(F32)
        else:
            one, other = refs[0][...].astype(F32), refs[1][...].astype(F32)
            total = total + jnp.where(t_ref[0] == choose, one, other)
        out_ref[...] = total.astype(dtype)

    out_cols = whole if whole else (2 if half is None else 4) * width
    return pl.pallas_call(
        kernel,
        grid_spec=pltpu.PrefetchScalarGridSpec(
            num_scalar_prefetch=1,
            grid=(2, per),
            in_specs=specs,
            out_specs=pl.BlockSpec((count, COLS), spread if whole else packed),
        ),
        out_shape=jax.ShapeDtypeStruct((count, out_cols), dtype),
        input_output_aliases=aliases,
        compiler_params=pltpu.CompilerParams(vmem_limit_bytes=VMEM),
        cost_estimate=pl.CostEstimate(
            flops=4 * count * depth * width, bytes_accessed=4 * depth * width + 8 * count * width, transcendentals=0
        ),
    )(ti, *operands)


def plane_product(ti, gathered, shards):
    m, _ = gathered.shape
    n = len(shards)
    depth, cols = shards[0][0].shape
    tm = min(512, m)

    def kernel(t_ref, *refs):
        rows_refs, shard_refs = refs[:n], refs[n : 3 * n]
        out_ref, held, sem = refs[3 * n :]
        first = pl.program_id(0) == 0
        end = jnp.logical_or(t_ref[0] == 0, t_ref[0] == n - 1)

        @pl.when(jnp.logical_and(first, end))
        def _():
            for d in range(n):
                pltpu.make_async_copy(shard_refs[2 * d], held.at[d], sem.at[d]).start()

        @pl.when(jnp.logical_and(first, jnp.logical_not(end)))
        def _():
            for d in range(n):
                pltpu.make_async_copy(shard_refs[2 * d + 1], held.at[d], sem.at[d]).start()

        acc = jnp.zeros((tm, cols), F32)
        for d in range(n):

            @pl.when(first)
            def _():
                pltpu.make_async_copy(shard_refs[2 * d], held.at[d], sem.at[d]).wait()

            acc = acc + jnp.dot(rows_refs[d][...], held[d], preferred_element_type=F32)
        out_ref[...] = acc.astype(BF16)

    return pl.pallas_call(
        kernel,
        grid_spec=pltpu.PrefetchScalarGridSpec(
            num_scalar_prefetch=1,
            grid=(m // tm,),
            in_specs=[pl.BlockSpec((tm, depth), lambda i, t, d=d: (i, t[0] ^ d)) for d in range(n)]
            + [pl.BlockSpec(memory_space=pl.ANY)] * (2 * n),
            out_specs=pl.BlockSpec((tm, cols), lambda i, t: (i, 0)),
            scratch_shapes=[pltpu.VMEM((n, depth, cols), BF16), pltpu.SemaphoreType.DMA((n,))],
        ),
        out_shape=jax.ShapeDtypeStruct((m, cols), BF16),
        compiler_params=pltpu.CompilerParams(vmem_limit_bytes=VMEM),
        cost_estimate=pl.CostEstimate(
            flops=2 * m * depth * cols * n,
            bytes_accessed=(2 * m * depth + 2 * depth * cols) * n + 2 * m * cols,
            transcendentals=0,
        ),
    )(ti, *[gathered] * n, *[ref for pair in shards for ref in pair])


def add_arrived(own, arrived, width, feat, into):
    count = own.shape[0]
    step, per = feat // COLS, width // COLS
    packed = lambda b, k: (0, b * per + k)
    spread = lambda b, k: (0, jnp.where(b < 2, b + 1, (b - 2) * 3) * step + k)

    def kernel(own_ref, one_ref, other_ref, into_ref, out_ref):
        out_ref[...] = (own_ref[...] + one_ref[...].astype(F32) + other_ref[...].astype(F32)).astype(BF16)

    return pl.pallas_call(
        kernel,
        grid=(4, per),
        in_specs=[pl.BlockSpec((count, COLS), packed)] * 3 + [pl.BlockSpec(memory_space=pl.ANY)],
        out_specs=pl.BlockSpec((count, COLS), spread),
        out_shape=jax.ShapeDtypeStruct(into.shape, BF16),
        input_output_aliases={3: 0},
        cost_estimate=pl.CostEstimate(flops=8 * count * width, bytes_accessed=40 * count * width, transcendentals=0),
    )(own, *arrived, into)


def plane_finish(ti, back, low, up_plane, feat, width, into, h):
    parts, tile, cols = back.shape
    per = (feat - width) // cols
    rank = low.shape[-1]

    given = [] if into is None else [into]

    def kernel(t_ref, back_ref, low_ref, up_ref, *refs):
        out_ref = refs[-1]
        delta = jnp.dot(low_ref[...], up_ref[...], preferred_element_type=F32).astype(BF16)
        out_ref[...] = (back_ref[...].astype(F32) + delta.astype(F32)).astype(BF16)

    return pl.pallas_call(
        kernel,
        grid_spec=pltpu.PrefetchScalarGridSpec(
            num_scalar_prefetch=1,
            grid=(parts // per, per),
            in_specs=[
                pl.BlockSpec((None, tile, cols), lambda j, k, t: (j * per + k, 0, 0)),
                pl.BlockSpec((None, None, tile, rank), lambda j, k, t: (t[0], h, 0, 0)),
                pl.BlockSpec((None, None, rank, cols), lambda j, k, t: (j, h, 0, k)),
            ]
            + [pl.BlockSpec(memory_space=pl.ANY)] * len(given),
            out_specs=pl.BlockSpec((tile, cols), lambda j, k, t: (h, j * (feat // cols) + width // cols + k)),
        ),
        out_shape=jax.ShapeDtypeStruct((low.shape[1] * tile, low.shape[0] * feat), BF16),
        input_output_aliases={4: 0} if given else {},
        compiler_params=pltpu.CompilerParams(vmem_limit_bytes=VMEM),
        cost_estimate=pl.CostEstimate(
            flops=2 * parts * tile * cols * rank, bytes_accessed=5 * parts * tile * cols, transcendentals=0
        ),
    )(ti, back, low, up_plane, *given)


def tile_slot(t, i, place):
    ids, slot_of, meta = t
    last = ids.shape[0] // TILE - 1
    return slot_of[ids[jnp.minimum(place * meta[2] + i, last) * TILE]]


def held_index(t, slot, count):
    return jnp.clip(slot - t[2][0] * count, 0, count - 1)


def map_call(kernel, scalars, grid, in_specs, out_specs, out_shape, nbytes, flops=0):
    return pl.pallas_call(
        kernel,
        grid_spec=pltpu.PrefetchScalarGridSpec(
            num_scalar_prefetch=3, grid=grid, in_specs=in_specs, out_specs=out_specs
        ),
        out_shape=out_shape,
        compiler_params=pltpu.CompilerParams(vmem_limit_bytes=VMEM),
        cost_estimate=pl.CostEstimate(flops=flops, bytes_accessed=nbytes, transcendentals=0),
    )


def maps_for_mate(scalars, bank, tiles, rows=None):
    count, rank, feat = bank.shape

    def at(h):
        return lambda i, *t: (held_index(t, tile_slot(t, i, t[2][0] ^ (1 + 2 * h)), count), 0, 0)

    in_specs = [pl.BlockSpec((None, rank, feat), at(h)) for h in range(2)]
    out_specs = [pl.BlockSpec((2, None, rank, feat), lambda i, *t: (0, i, 0, 0))]
    out_shape = [jax.ShapeDtypeStruct((2, tiles, rank, feat), BF16)]
    operands = [bank, bank]
    if rows is not None:
        n = rows.shape[1] // feat
        some = rows.shape[0] // tiles
        in_specs.append(pl.BlockSpec((some, n * feat), lambda i, *t: (i, 0)))
        out_specs.append(pl.BlockSpec((n, some, feat), lambda i, *t: (0, i, 0)))
        out_shape.append(jax.ShapeDtypeStruct((n, rows.shape[0], feat), BF16))
        operands.append(rows)

    def kernel(ids, slot_of, meta, one_ref, other_ref, *refs):
        out_ref = refs[0] if rows is None else refs[1]
        out_ref[0] = one_ref[...]
        out_ref[1] = other_ref[...]
        if rows is not None:
            for j in range(n):
                refs[2][j] = refs[0][:, j * feat : (j + 1) * feat]

    out = map_call(
        kernel, scalars, (tiles,), in_specs, out_specs, out_shape, 8 * tiles * rank * feat
    )(*scalars, *operands)
    return [out[0].reshape(2 * tiles, rank, feat)] + list(out[1:])


def maps_for_far(scalars, bank, got, tiles):
    count, rank, feat = bank.shape

    def at(i, *t):
        return (held_index(t, tile_slot(t, i, t[2][0] ^ 2), count), 0, 0)

    def kernel(ids, slot_of, meta, bank_ref, got_ref, out_ref):
        slot = tile_slot((ids, slot_of, meta), pl.program_id(0), meta[0] ^ 2)
        mine = slot // count == meta[0]

        @pl.when(mine)
        def _():
            out_ref[...] = bank_ref[...]

        @pl.when(jnp.logical_not(mine))
        def _():
            out_ref[...] = got_ref[...]

    return map_call(
        kernel, scalars, (tiles,),
        [pl.BlockSpec((1, rank, feat), at), pl.BlockSpec((1, rank, feat), lambda i, *t: (tiles + i, 0, 0))],
        pl.BlockSpec((1, rank, feat), lambda i, *t: (i, 0, 0)),
        jax.ShapeDtypeStruct((tiles, rank, feat), BF16),
        6 * tiles * rank * feat,
    )(*scalars, bank, got)


def own_specs(bank, tiles):
    count, rank, feat = bank.shape

    def at(i, *t):
        return (held_index(t, tile_slot(t, i, t[2][0]), count), 0, 0)

    tile = lambda i, *t: (i, 0, 0)
    block = (None, rank, feat)
    return [pl.BlockSpec(block, at), pl.BlockSpec(block, tile), pl.BlockSpec(block, tile)]


def with_own(scalar_refs, count, refs, use):
    meta = scalar_refs[2]
    place = tile_slot(scalar_refs, pl.program_id(0), meta[0]) // count
    here, mate = place == meta[0], place == (meta[0] ^ 1)
    far = jnp.logical_not(jnp.logical_or(here, mate))
    for flag, ref in zip((here, mate, far), refs):
        pl.when(flag)(lambda ref=ref: use(ref))


def low_parts(scalars, rows, bank, got, far, tiles):
    count, rank, feat = bank.shape

    def kernel(ids, slot_of, meta, rows_ref, bank_ref, got_ref, far_ref, out_ref):
        def use(ref):
            out_ref[...] = lax.dot_general(
                rows_ref[...], ref[...], (((1,), (1,)), ((), ())), preferred_element_type=F32
            )

        with_own((ids, slot_of, meta), count, (bank_ref, got_ref, far_ref), use)

    return map_call(
        kernel, scalars, (tiles,),
        [pl.BlockSpec((None, TILE, feat), lambda i, *t: (i, 0, 0))] + own_specs(bank, tiles),
        pl.BlockSpec((None, TILE, rank), lambda i, *t: (i, 0, 0)),
        jax.ShapeDtypeStruct((tiles, TILE, rank), F32),
        (6 * rank + 2 * TILE) * tiles * feat, 2 * tiles * TILE * rank * feat,
    )(*scalars, rows, bank, got, far)


def adapter_terms(scalars, low, bank, got, far, tiles, width):
    count, rank, feat = bank.shape

    def kernel(ids, slot_of, meta, low_ref, bank_ref, got_ref, far_ref, term_ref, up_ref):
        def use(ref):
            term_ref[...] = jnp.dot(low_ref[...], ref[:, :width], preferred_element_type=F32).astype(BF16)
            up_ref[...] = ref[:, width:]

        with_own((ids, slot_of, meta), count, (bank_ref, got_ref, far_ref), use)

    tile = lambda i, *t: (i, 0, 0)
    return map_call(
        kernel, scalars, (tiles,),
        [pl.BlockSpec((None, TILE, rank), tile)] + own_specs(bank, tiles),
        [pl.BlockSpec((None, TILE, width), tile), pl.BlockSpec((None, rank, feat - width), tile)],
        [
            jax.ShapeDtypeStruct((tiles, TILE, width), BF16),
            jax.ShapeDtypeStruct((tiles, rank, feat - width), BF16),
        ],
        (7 * rank + TILE) * tiles * feat, 2 * tiles * TILE * rank * width,
    )(*scalars, low, bank, got, far)


SPLIT = 2


def line_body(x, w, down, up, ids, slot_of):
    stores = lax.axis_size("store")
    members = lax.axis_size("groups") * stores
    n = 4
    si = lax.axis_index("store")
    ti = lax.axis_index("tensor")
    pi = lax.axis_index("groups") * stores + si
    scalar = ti.astype(jnp.int32).reshape(1)
    rows = x.shape[0]
    feat = w.shape[0]
    own_tiles = rows // TILE
    tiles = n * own_tiles
    rank = down.shape[1]
    plane_width = feat // SPLIT
    width = feat - plane_width
    ends_out = [(0, 1), (3, 2)]
    inward_right, inward_left = [(0, 1), (1, 2)], [(3, 2), (2, 1)]
    middle = [(1, 2), (2, 1)]
    to_ends = [(1, 0), (2, 3)]
    send = lambda v, pairs: lax.ppermute(v, "tensor", pairs)

    meta = jnp.stack([si, ti, jnp.int32(tiles)]).astype(jnp.int32)
    scalars = (ids, slot_of, meta)
    after = lambda value, *others: lax.optimization_barrier((value, *others))[0]

    down_send, blocks = maps_for_mate(scalars, down, tiles, x)
    blocks = lax.all_to_all(blocks, "tensor", split_axis=0, concat_axis=0, tiled=True)
    down_got = xor_perm(down_send, "store", 1)
    down_to_far = maps_for_far(scalars, down, down_got, tiles)
    down_far = xor_perm(down_to_far, "store", 2)
    (up_send,) = maps_for_mate(after(scalars, down_send), up, tiles)
    up_got = xor_perm(up_send, "store", 1)
    up_far = xor_perm(maps_for_far(scalars, up, up_got, tiles), "store", 2)

    cols = plane_width * n // members
    per = plane_width // cols
    w_own = lax.dynamic_slice_in_dim(w, (pi // per) * feat + width + (pi % per) * cols, cols, 1)
    w_near = xor_perm(w_own, "tensor", 1)
    w_mid = send(w_own, middle)

    gathered = []
    for h in range(own_tiles):
        half = after(x[h * TILE : (h + 1) * TILE], up_far, down_far, blocks)
        gathered.append(lax.all_gather(half, PLANE, axis=0, tiled=True))

    low = low_parts(scalars, blocks.reshape(tiles, TILE, feat), down, down_got, down_far, tiles)
    low = low + xor_perm(low.astype(BF16), "tensor", 1).astype(F32)
    low = (low + xor_perm(low.astype(BF16), "tensor", 2).astype(F32)).astype(BF16)
    terms, up_plane = adapter_terms(scalars, low, up, up_got, up_far, tiles, width)
    terms = terms.reshape(n, rows, width)
    def partial(chunk, d, arrived=(), term=True, rows_in=blocks, **kw):
        return chunk_partial(scalar, chunk, feat, width, rows_in, w, term, terms, d, arrived, **kw)

    inner, outer = (1, 1), (0, 3)
    early = partial(inner, 3, term=False)
    w_end2 = send(w_mid, to_ends)
    w_mid2 = send(after(w_near, low, early), middle)
    late = partial(outer, 3)
    first = [send(early, ends_out), send(late, ends_out)]
    seconds, own, to_near, to_mid = [], None, None, None
    for half, (chunk, came) in enumerate(zip((inner, outer), first)):
        own = partial(chunk, 0, rows_in=after(blocks, *(seconds or [late])), half=half, into=own, dtype=F32)
        second = partial(chunk, 2, (came,), rows_in=after(blocks, own))
        seconds.append(second)
        right, left = send(second, inward_right), send(second, inward_left)
        to_near = partial(chunk, 1, (left, right), choose=1, half=half, into=to_near)
        to_mid = partial(chunk, 3, (right, left), choose=1, half=half, into=to_mid)
    lasts = (to_near, to_mid)
    arrived = (xor_perm(to_near, "tensor", 1), send(to_mid, middle))

    w_end3 = send(after(w_mid2, *seconds), to_ends)
    up_plane = lax.all_to_all(
        up_plane.reshape(n, own_tiles, rank, plane_width), "tensor", split_axis=0, concat_axis=0, tiled=True
    )
    shards = [(w_own, w_own), (w_near, w_near), (w_end2, w_mid2), (w_end3, w_mid)]
    waits = [lasts, lasts]
    back = []
    for h in range(own_tiles):
        total = plane_product(scalar, after(gathered[h], *waits[min(h, 1)]), shards)
        back.append(lax.all_to_all(total.reshape(members, TILE, cols), PLANE, split_axis=0, concat_axis=0, tiled=True))

    low = low.reshape(n, own_tiles, TILE, rank)
    out = None
    for h in range(own_tiles):
        if h == own_tiles - 1:
            out = add_arrived(own, arrived, width, feat, out)
        out = plane_finish(scalar, back[h], low, up_plane, feat, width, out, h)
    return out


def body(x, w, down, up, ids, slot_of):
    line = lax.axis_size("tensor") == 4 and lax.axis_size("store") == 4 and lax.axis_size("groups") == 2
    line = line and x.shape[0] % TILE == 0 and x.shape[0] > TILE and w.shape[0] % (2 * COLS) == 0
    return (line_body if line else general_body)(x, w, down, up, ids, slot_of)


def solution(mesh):
    return jax.shard_map(
        body,
        mesh=mesh,
        in_specs=(
            P(("groups", "store", "tensor"), None),
            P("tensor", None),
            P("store", None, "tensor"),
            P("store", None, "tensor"),
            P("groups"),
            P(),
        ),
        out_specs=P(("groups", "store", "tensor"), None),
        check_vma=False,
    )
```

```python
import jax
import jax.numpy as jnp
from jax import lax
from jax.experimental import pallas as pl
from jax.experimental.pallas import tpu as pltpu
from jax.sharding import PartitionSpec as P

TILE = 128
F32 = jnp.float32
BF16 = jnp.bfloat16


def xor_perm(x, axis, d):
    return lax.ppermute(x, axis, [(i, i ^ d) for i in range(lax.axis_size(axis))])


def pick(bank, first, slots):
    count = bank.shape[0]
    held = (slots >= first) & (slots < first + count)
    return jnp.take(bank, jnp.clip(slots - first, 0, count - 1), axis=0), held[:, None, None]


def fetch_maps(bank, slots, me):
    n = lax.axis_size("store")
    first = me * bank.shape[0]
    if n != 4:
        return jnp.take(lax.all_gather(bank, "store", axis=0, tiled=True), slots[me], axis=0)
    own, own_held = pick(bank, first, slots[me])
    mate, _ = pick(bank, first, slots[me ^ 1])
    far, far_held = pick(bank, first, slots[me ^ 2])
    far_mate, _ = pick(bank, first, slots[me ^ 3])
    from_mate = xor_perm(mate, "store", 1)
    far_from_mate = xor_perm(far_mate, "store", 1)
    from_far = xor_perm(jnp.where(far_held, far, far_from_mate), "store", 2)
    mate_first = (me ^ 1) * bank.shape[0]
    mate_held = (slots[me] >= mate_first) & (slots[me] < mate_first + bank.shape[0])
    return jnp.where(own_held, own, jnp.where(mate_held[:, None, None], from_mate, from_far))


def general_body(x, w, down, up, ids, slot_of):
    stores = lax.axis_size("store")
    n = lax.axis_size("tensor")
    si = lax.axis_index("store")
    ti = lax.axis_index("tensor")
    rows = x.shape[0]
    feat = w.shape[0]
    slots = slot_of[ids.reshape(-1, TILE)[:, 0]].reshape(stores, -1)
    tiles = slots.shape[1]
    blocks = x.reshape(rows, n, feat).transpose(1, 0, 2)
    blocks = lax.all_to_all(blocks, "tensor", split_axis=0, concat_axis=0, tiled=True)
    local = blocks.reshape(n * rows, feat)
    tile_down = fetch_maps(down, slots, si)
    tile_up = fetch_maps(up, slots, si)
    low = jnp.einsum("tnd,trd->tnr", local.reshape(tiles, TILE, feat), tile_down, preferred_element_type=F32)
    low = lax.psum(low.astype(BF16), "tensor")
    delta = jnp.einsum("tnr,trd->tnd", low, tile_up, preferred_element_type=F32).reshape(n * rows, feat)
    part = jnp.dot(local, w, preferred_element_type=F32).astype(BF16)
    w_own = lax.dynamic_slice_in_dim(w, ti * feat, feat, 1)
    own = jnp.dot(local, w_own, preferred_element_type=F32) + delta
    part = lax.dynamic_update_slice_in_dim(part, own.astype(BF16), ti * feat, 1)
    return lax.psum_scatter(part, "tensor", scatter_dimension=0, tiled=True)


PLANE = ("groups", "store")
COLS = 1024
VMEM = 48 * 1024 * 1024


def chunk_partial(ti, blocks, feat, width, rows, w, term, terms, d, arrived, whole=None, into=None, choose=None, half=None, dtype=BF16):
    first, stride = blocks
    _, count, depth = rows.shape
    per = width // COLS
    step = feat // COLS
    packed = lambda b, k, t: (0, ((half or 0) * 2 + b) * per + k)
    spread = lambda b, k, t: (0, (first + b * stride) * step + k)
    operands = [rows, w]
    specs = [pl.BlockSpec((None, count, depth), lambda b, k, t: (t[0] ^ d, 0, 0)), pl.BlockSpec((depth, COLS), spread)]
    if term:
        operands.append(terms)
        specs.append(pl.BlockSpec((None, count, COLS), lambda b, k, t: (t[0] ^ d, 0, k)))
    for piece in arrived:
        operands.append(piece)
        specs.append(pl.BlockSpec((count, COLS), lambda b, k, t: (0, b * per + k)))
    aliases = {}
    if into is not None:
        aliases = {1 + len(operands): 0}
        operands.append(into)
        specs.append(pl.BlockSpec(memory_space=pl.ANY))

    def kernel(t_ref, rows_ref, w_ref, *refs):
        total = jnp.dot(rows_ref[...], w_ref[...], preferred_element_type=F32)
        refs, out_ref = list(refs[:-1]), refs[-1]
        if term:
            own = first + pl.program_id(0) * stride == t_ref[0]
            total = total + jnp.where(own, refs.pop(0)[...].astype(F32), 0.0)
        if choose is None:
            for ref in refs[: len(arrived)]:
                total = total + ref[...].astype(F32)
        else:
            one, other = refs[0][...].astype(F32), refs[1][...].astype(F32)
            total = total + jnp.where(t_ref[0] == choose, one, other)
        out_ref[...] = total.astype(dtype)

    out_cols = whole if whole else (2 if half is None else 4) * width
    return pl.pallas_call(
        kernel,
        grid_spec=pltpu.PrefetchScalarGridSpec(
            num_scalar_prefetch=1,
            grid=(2, per),
            in_specs=specs,
            out_specs=pl.BlockSpec((count, COLS), spread if whole else packed),
        ),
        out_shape=jax.ShapeDtypeStruct((count, out_cols), dtype),
        input_output_aliases=aliases,
        compiler_params=pltpu.CompilerParams(vmem_limit_bytes=VMEM),
        cost_estimate=pl.CostEstimate(
            flops=4 * count * depth * width, bytes_accessed=4 * depth * width + 8 * count * width, transcendentals=0
        ),
    )(ti, *operands)


def plane_product(ti, gathered, shards):
    m, _ = gathered.shape
    n = len(shards)
    depth, cols = shards[0][0].shape
    tm = min(512, m)

    def kernel(t_ref, *refs):
        rows_refs, shard_refs = refs[:n], refs[n : 3 * n]
        out_ref, held, sem = refs[3 * n :]
        first = pl.program_id(0) == 0
        end = jnp.logical_or(t_ref[0] == 0, t_ref[0] == n - 1)

        @pl.when(jnp.logical_and(first, end))
        def _():
            for d in range(n):
                pltpu.make_async_copy(shard_refs[2 * d], held.at[d], sem.at[d]).start()

        @pl.when(jnp.logical_and(first, jnp.logical_not(end)))
        def _():
            for d in range(n):
                pltpu.make_async_copy(shard_refs[2 * d + 1], held.at[d], sem.at[d]).start()

        acc = jnp.zeros((tm, cols), F32)
        for d in range(n):

            @pl.when(first)
            def _():
                pltpu.make_async_copy(shard_refs[2 * d], held.at[d], sem.at[d]).wait()

            acc = acc + jnp.dot(rows_refs[d][...], held[d], preferred_element_type=F32)
        out_ref[...] = acc.astype(BF16)

    return pl.pallas_call(
        kernel,
        grid_spec=pltpu.PrefetchScalarGridSpec(
            num_scalar_prefetch=1,
            grid=(m // tm,),
            in_specs=[pl.BlockSpec((tm, depth), lambda i, t, d=d: (i, t[0] ^ d)) for d in range(n)]
            + [pl.BlockSpec(memory_space=pl.ANY)] * (2 * n),
            out_specs=pl.BlockSpec((tm, cols), lambda i, t: (i, 0)),
            scratch_shapes=[pltpu.VMEM((n, depth, cols), BF16), pltpu.SemaphoreType.DMA((n,))],
        ),
        out_shape=jax.ShapeDtypeStruct((m, cols), BF16),
        compiler_params=pltpu.CompilerParams(vmem_limit_bytes=VMEM),
        cost_estimate=pl.CostEstimate(
            flops=2 * m * depth * cols * n,
            bytes_accessed=(2 * m * depth + 2 * depth * cols) * n + 2 * m * cols,
            transcendentals=0,
        ),
    )(ti, *[gathered] * n, *[ref for pair in shards for ref in pair])


def add_arrived(own, arrived, width, feat, into):
    count = own.shape[0]
    step, per = feat // COLS, width // COLS
    packed = lambda b, k: (0, b * per + k)
    spread = lambda b, k: (0, jnp.where(b < 2, b + 1, (b - 2) * 3) * step + k)

    def kernel(own_ref, one_ref, other_ref, into_ref, out_ref):
        out_ref[...] = (own_ref[...] + one_ref[...].astype(F32) + other_ref[...].astype(F32)).astype(BF16)

    return pl.pallas_call(
        kernel,
        grid=(4, per),
        in_specs=[pl.BlockSpec((count, COLS), packed)] * 3 + [pl.BlockSpec(memory_space=pl.ANY)],
        out_specs=pl.BlockSpec((count, COLS), spread),
        out_shape=jax.ShapeDtypeStruct(into.shape, BF16),
        input_output_aliases={3: 0},
        cost_estimate=pl.CostEstimate(flops=8 * count * width, bytes_accessed=40 * count * width, transcendentals=0),
    )(own, *arrived, into)


def plane_finish(ti, back, low, up_plane, feat, width, into, h):
    parts, tile, cols = back.shape
    per = (feat - width) // cols
    rank = low.shape[-1]

    given = [] if into is None else [into]

    def kernel(t_ref, back_ref, low_ref, up_ref, *refs):
        out_ref = refs[-1]
        delta = jnp.dot(low_ref[...], up_ref[...], preferred_element_type=F32).astype(BF16)
        out_ref[...] = (back_ref[...].astype(F32) + delta.astype(F32)).astype(BF16)

    return pl.pallas_call(
        kernel,
        grid_spec=pltpu.PrefetchScalarGridSpec(
            num_scalar_prefetch=1,
            grid=(parts // per, per),
            in_specs=[
                pl.BlockSpec((None, tile, cols), lambda j, k, t: (j * per + k, 0, 0)),
                pl.BlockSpec((None, None, tile, rank), lambda j, k, t: (t[0], h, 0, 0)),
                pl.BlockSpec((None, None, rank, cols), lambda j, k, t: (j, h, 0, k)),
            ]
            + [pl.BlockSpec(memory_space=pl.ANY)] * len(given),
            out_specs=pl.BlockSpec((tile, cols), lambda j, k, t: (h, j * (feat // cols) + width // cols + k)),
        ),
        out_shape=jax.ShapeDtypeStruct((low.shape[1] * tile, low.shape[0] * feat), BF16),
        input_output_aliases={4: 0} if given else {},
        compiler_params=pltpu.CompilerParams(vmem_limit_bytes=VMEM),
        cost_estimate=pl.CostEstimate(
            flops=2 * parts * tile * cols * rank, bytes_accessed=5 * parts * tile * cols, transcendentals=0
        ),
    )(ti, back, low, up_plane, *given)


def tile_slot(t, i, place):
    ids, slot_of, meta = t
    last = ids.shape[0] // TILE - 1
    return slot_of[ids[jnp.minimum(place * meta[2] + i, last) * TILE]]


def held_index(t, slot, count):
    return jnp.clip(slot - t[2][0] * count, 0, count - 1)


def map_call(kernel, scalars, grid, in_specs, out_specs, out_shape, nbytes, flops=0):
    return pl.pallas_call(
        kernel,
        grid_spec=pltpu.PrefetchScalarGridSpec(
            num_scalar_prefetch=3, grid=grid, in_specs=in_specs, out_specs=out_specs
        ),
        out_shape=out_shape,
        compiler_params=pltpu.CompilerParams(vmem_limit_bytes=VMEM),
        cost_estimate=pl.CostEstimate(flops=flops, bytes_accessed=nbytes, transcendentals=0),
    )


def maps_for_mate(scalars, bank, tiles, rows=None):
    count, rank, feat = bank.shape

    def at(h):
        return lambda i, *t: (held_index(t, tile_slot(t, i, t[2][0] ^ (1 + 2 * h)), count), 0, 0)

    in_specs = [pl.BlockSpec((None, rank, feat), at(h)) for h in range(2)]
    out_specs = [pl.BlockSpec((2, None, rank, feat), lambda i, *t: (0, i, 0, 0))]
    out_shape = [jax.ShapeDtypeStruct((2, tiles, rank, feat), BF16)]
    operands = [bank, bank]
    if rows is not None:
        n = rows.shape[1] // feat
        some = rows.shape[0] // tiles
        in_specs.append(pl.BlockSpec((some, n * feat), lambda i, *t: (i, 0)))
        out_specs.append(pl.BlockSpec((n, some, feat), lambda i, *t: (0, i, 0)))
        out_shape.append(jax.ShapeDtypeStruct((n, rows.shape[0], feat), BF16))
        operands.append(rows)

    def kernel(ids, slot_of, meta, one_ref, other_ref, *refs):
        out_ref = refs[0] if rows is None else refs[1]
        out_ref[0] = one_ref[...]
        out_ref[1] = other_ref[...]
        if rows is not None:
            for j in range(n):
                refs[2][j] = refs[0][:, j * feat : (j + 1) * feat]

    out = map_call(
        kernel, scalars, (tiles,), in_specs, out_specs, out_shape, 8 * tiles * rank * feat
    )(*scalars, *operands)
    return [out[0].reshape(2 * tiles, rank, feat)] + list(out[1:])


def maps_for_far(scalars, bank, got, tiles):
    count, rank, feat = bank.shape

    def at(i, *t):
        return (held_index(t, tile_slot(t, i, t[2][0] ^ 2), count), 0, 0)

    def kernel(ids, slot_of, meta, bank_ref, got_ref, out_ref):
        slot = tile_slot((ids, slot_of, meta), pl.program_id(0), meta[0] ^ 2)
        mine = slot // count == meta[0]

        @pl.when(mine)
        def _():
            out_ref[...] = bank_ref[...]

        @pl.when(jnp.logical_not(mine))
        def _():
            out_ref[...] = got_ref[...]

    return map_call(
        kernel, scalars, (tiles,),
        [pl.BlockSpec((1, rank, feat), at), pl.BlockSpec((1, rank, feat), lambda i, *t: (tiles + i, 0, 0))],
        pl.BlockSpec((1, rank, feat), lambda i, *t: (i, 0, 0)),
        jax.ShapeDtypeStruct((tiles, rank, feat), BF16),
        6 * tiles * rank * feat,
    )(*scalars, bank, got)


def own_specs(bank, tiles):
    count, rank, feat = bank.shape

    def at(i, *t):
        return (held_index(t, tile_slot(t, i, t[2][0]), count), 0, 0)

    tile = lambda i, *t: (i, 0, 0)
    block = (None, rank, feat)
    return [pl.BlockSpec(block, at), pl.BlockSpec(block, tile), pl.BlockSpec(block, tile)]


def with_own(scalar_refs, count, refs, use):
    meta = scalar_refs[2]
    place = tile_slot(scalar_refs, pl.program_id(0), meta[0]) // count
    here, mate = place == meta[0], place == (meta[0] ^ 1)
    far = jnp.logical_not(jnp.logical_or(here, mate))
    for flag, ref in zip((here, mate, far), refs):
        pl.when(flag)(lambda ref=ref: use(ref))


def low_parts(scalars, rows, bank, got, far, tiles):
    count, rank, feat = bank.shape

    def kernel(ids, slot_of, meta, rows_ref, bank_ref, got_ref, far_ref, out_ref):
        def use(ref):
            out_ref[...] = lax.dot_general(
                rows_ref[...], ref[...], (((1,), (1,)), ((), ())), preferred_element_type=F32
            )

        with_own((ids, slot_of, meta), count, (bank_ref, got_ref, far_ref), use)

    return map_call(
        kernel, scalars, (tiles,),
        [pl.BlockSpec((None, TILE, feat), lambda i, *t: (i, 0, 0))] + own_specs(bank, tiles),
        pl.BlockSpec((None, TILE, rank), lambda i, *t: (i, 0, 0)),
        jax.ShapeDtypeStruct((tiles, TILE, rank), F32),
        (6 * rank + 2 * TILE) * tiles * feat, 2 * tiles * TILE * rank * feat,
    )(*scalars, rows, bank, got, far)


def adapter_terms(scalars, low, bank, got, far, tiles, width):
    count, rank, feat = bank.shape

    def kernel(ids, slot_of, meta, low_ref, bank_ref, got_ref, far_ref, term_ref, up_ref):
        def use(ref):
            term_ref[...] = jnp.dot(low_ref[...], ref[:, :width], preferred_element_type=F32).astype(BF16)
            up_ref[...] = ref[:, width:]

        with_own((ids, slot_of, meta), count, (bank_ref, got_ref, far_ref), use)

    tile = lambda i, *t: (i, 0, 0)
    return map_call(
        kernel, scalars, (tiles,),
        [pl.BlockSpec((None, TILE, rank), tile)] + own_specs(bank, tiles),
        [pl.BlockSpec((None, TILE, width), tile), pl.BlockSpec((None, rank, feat - width), tile)],
        [
            jax.ShapeDtypeStruct((tiles, TILE, width), BF16),
            jax.ShapeDtypeStruct((tiles, rank, feat - width), BF16),
        ],
        (7 * rank + TILE) * tiles * feat, 2 * tiles * TILE * rank * width,
    )(*scalars, low, bank, got, far)


SPLIT = 2


def line_body(x, w, down, up, ids, slot_of):
    stores = lax.axis_size("store")
    members = lax.axis_size("groups") * stores
    n = 4
    si = lax.axis_index("store")
    ti = lax.axis_index("tensor")
    pi = lax.axis_index("groups") * stores + si
    scalar = ti.astype(jnp.int32).reshape(1)
    rows = x.shape[0]
    feat = w.shape[0]
    own_tiles = rows // TILE
    tiles = n * own_tiles
    rank = down.shape[1]
    plane_width = feat // SPLIT
    width = feat - plane_width
    ends_out = [(0, 1), (3, 2)]
    inward_right, inward_left = [(0, 1), (1, 2)], [(3, 2), (2, 1)]
    middle = [(1, 2), (2, 1)]
    to_ends = [(1, 0), (2, 3)]
    send = lambda v, pairs: lax.ppermute(v, "tensor", pairs)

    meta = jnp.stack([si, ti, jnp.int32(tiles)]).astype(jnp.int32)
    scalars = (ids, slot_of, meta)
    after = lambda value, *others: lax.optimization_barrier((value, *others))[0]

    down_send, blocks = maps_for_mate(scalars, down, tiles, x)
    blocks = lax.all_to_all(blocks, "tensor", split_axis=0, concat_axis=0, tiled=True)
    down_got = xor_perm(down_send, "store", 1)
    down_to_far = maps_for_far(scalars, down, down_got, tiles)
    down_far = xor_perm(down_to_far, "store", 2)
    (up_send,) = maps_for_mate(after(scalars, down_send), up, tiles)
    up_got = xor_perm(up_send, "store", 1)
    up_far = xor_perm(maps_for_far(scalars, up, up_got, tiles), "store", 2)

    cols = plane_width * n // members
    per = plane_width // cols
    w_own = lax.dynamic_slice_in_dim(w, (pi // per) * feat + width + (pi % per) * cols, cols, 1)
    w_near = xor_perm(w_own, "tensor", 1)
    w_mid = send(w_own, middle)

    gathered = []
    for h in range(own_tiles):
        half = after(x[h * TILE : (h + 1) * TILE], up_far, down_far, blocks)
        gathered.append(lax.all_gather(half, PLANE, axis=0, tiled=True))

    low = low_parts(scalars, blocks.reshape(tiles, TILE, feat), down, down_got, down_far, tiles)
    low = low + xor_perm(low.astype(BF16), "tensor", 1).astype(F32)
    low = (low + xor_perm(low.astype(BF16), "tensor", 2).astype(F32)).astype(BF16)
    terms, up_plane = adapter_terms(scalars, low, up, up_got, up_far, tiles, width)
    terms = terms.reshape(n, rows, width)
    def partial(chunk, d, arrived=(), term=True, rows_in=blocks, **kw):
        return chunk_partial(scalar, chunk, feat, width, rows_in, w, term, terms, d, arrived, **kw)

    inner, outer = (1, 1), (0, 3)
    early = partial(inner, 3, term=False)
    w_end2 = send(w_mid, to_ends)
    w_mid2 = send(after(w_near, low, early), middle)
    late = partial(outer, 3)
    first = [send(early, ends_out), send(late, ends_out)]
    seconds, own, to_near, to_mid = [], None, None, None
    for half, (chunk, came) in enumerate(zip((inner, outer), first)):
        own = partial(chunk, 0, rows_in=after(blocks, *(seconds or [late])), half=half, into=own, dtype=F32)
        second = partial(chunk, 2, (came,), rows_in=after(blocks, own))
        seconds.append(second)
        right, left = send(second, inward_right), send(second, inward_left)
        to_near = partial(chunk, 1, (left, right), choose=1, half=half, into=to_near)
        to_mid = partial(chunk, 3, (right, left), choose=1, half=half, into=to_mid)
    lasts = (to_near, to_mid)
    arrived = (xor_perm(to_near, "tensor", 1), send(to_mid, middle))

    w_end3 = send(after(w_mid2, *seconds), to_ends)
    up_plane = lax.all_to_all(
        up_plane.reshape(n, own_tiles, rank, plane_width), "tensor", split_axis=0, concat_axis=0, tiled=True
    )
    shards = [(w_own, w_own), (w_near, w_near), (w_end2, w_mid2), (w_end3, w_mid)]
    waits = [lasts, lasts]
    back = []
    for h in range(own_tiles):
        total = plane_product(scalar, after(gathered[h], *waits[min(h, 1)]), shards)
        back.append(lax.all_to_all(total.reshape(members, TILE, cols), PLANE, split_axis=0, concat_axis=0, tiled=True))

    low = low.reshape(n, own_tiles, TILE, rank)
    out = None
    for h in range(own_tiles):
        if h == own_tiles - 1:
            out = add_arrived(own, arrived, width, feat, out)
        out = plane_finish(scalar, back[h], low, up_plane, feat, width, out, h)
    return out


def body(x, w, down, up, ids, slot_of):
    line = lax.axis_size("tensor") == 4 and lax.axis_size("store") == 4 and lax.axis_size("groups") == 2
    line = line and x.shape[0] % TILE == 0 and x.shape[0] > TILE and w.shape[0] % (2 * COLS) == 0
    return (line_body if line else general_body)(x, w, down, up, ids, slot_of)


def solution(mesh):
    return jax.shard_map(
        body,
        mesh=mesh,
        in_specs=(
            P(("groups", "store", "tensor"), None),
            P("tensor", None),
            P("store", None, "tensor"),
            P("store", None, "tensor"),
            P("groups"),
            P(),
        ),
        out_specs=P(("groups", "store", "tensor"), None),
        check_vma=False,
    )
```
